512 devices in a mesh: row: 32 (over y, z_lo), col: 16 (over z_hi, x, core).
Axes of the slice: x: 4, y: 4, z: 16 (z_hi: 2, z_lo: 8; z = z_hi * 8 + z_lo), core: 2. Of those that a mesh axis runs over, the one named last changes fastest.
Arguments:
- blocks: bfloat16 [32, 16, 40, 128, 128], P('row', 'col'), may hold values from -2.5 to 2.5
- block_rows: int32 [32, 16, 40], P('row', 'col'), may hold values from -1 to 12, as said below
- block_cols: int32 [32, 16, 40], P('row', 'col'), may hold values from -1 to 25, as said below
Outputs:
- product: bfloat16 [32, 16, 40, 128, 128], P('row', 'col')
The draws below stay inside these ranges and needn't reach their ends.
Inputs may be any that keep to these rules, and one draw needn't show every extreme that they name: On each device the live slots name distinct (row, column) pairs; an empty slot has -1 in block_rows and block_cols alike, and slots are in no particular order. Each half of a device's block columns (the first 13 or the last 13) holds at least 10 and at most 20 stored blocks, and some half in the matrix holds exactly 20. `block_cols`: see block_rows: the same slots are live.
All inputs are finite; a program needn't handle non-finite values.
Results may differ from the reference program's by a relative error of at most 0.001.
Values may be sent and summed in bfloat16 or wider, within the bound.
A program may use at most 64 MiB of HBM per device.

```python
import jax
import jax.numpy as jnp
from jax import lax

BS = 128
BROW = 13
HALF = 20
SLOTS = 40
N_ROW = 32
N_COL = 16


def shuffled_cells(seed_key):
    return jax.random.permutation(seed_key, BROW * BROW)[:HALF]


def shuffled_slots(seed_key):
    return jax.random.permutation(seed_key, SLOTS)


def pattern(key):
    block_families = N_ROW * N_COL * 2
    counts = jax.random.randint(jax.random.fold_in(key, 101), (block_families,), HALF // 2, HALF + 1)
    chosen_group = jax.random.randint(jax.random.fold_in(key, 102), (), 0, block_families)
    counts = jnp.where(jnp.arange(block_families) == chosen_group, HALF, counts)
    picked = jax.vmap(shuffled_cells)(jax.random.split(jax.random.fold_in(key, 103), block_families))
    filled = jnp.arange(HALF)[None, :] < counts[:, None]
    column_side = (jnp.arange(block_families) % 2)[:, None]
    position_rows = jnp.where(filled, picked // BROW, -1).reshape(N_ROW * N_COL, SLOTS)
    slot_cols = jnp.where(filled, picked % BROW + column_side * BROW, -1).reshape(N_ROW * N_COL, SLOTS)
    slot_order = jax.vmap(shuffled_slots)(jax.random.split(jax.random.fold_in(key, 104), N_ROW * N_COL))
    position_rows = jnp.take_along_axis(position_rows, slot_order, axis=1)
    slot_cols = jnp.take_along_axis(slot_cols, slot_order, axis=1)
    return (position_rows.reshape(N_ROW, N_COL, SLOTS).astype(jnp.int32), slot_cols.reshape(N_ROW, N_COL, SLOTS).astype(jnp.int32))


def draw_block_rows(key, part):
    return pattern(key)[0]


def draw_block_cols(key, part):
    return pattern(key)[1]


def shard_levels(stream_key, shape, shards, smallest, largest):
    def one(dim, shards_of):
        heights = jax.random.uniform(jax.random.fold_in(jax.random.fold_in(stream_key, 6), dim), (shards_of,), jnp.float32, smallest / len(shards), largest / len(shards))
        return jnp.repeat(jnp.exp(heights), shape[dim] // shards_of).reshape((-1,) + (1,) * (len(shape) - dim - 1))

    gain = one(*shards[0])
    for cut in shards[1:]:
        gain = gain * one(*cut)
    return gain


def scatter_about(own_key, dims, scale, reach, cuts=(), kind=jnp.bfloat16):
    loudness = shard_levels(own_key, dims, cuts, -0.22, 0.18) if cuts else 1.0
    values = jax.random.normal(own_key, dims, jnp.float32) * scale * loudness
    return jnp.minimum(jnp.maximum(values, -reach), reach).astype(kind)


def setup_inputs(seed: int = 0) -> dict:
    key_of = jax.random.split(jax.random.key(seed), 4)
    blocks = scatter_about(key_of[0], (N_ROW, N_COL, SLOTS, BS, BS), (BS ** -0.25), 2.5, ((0, 32), (1, 16)))
    block_rows = draw_block_rows(jax.random.fold_in(key_of[3], 71), 0)
    block_cols = draw_block_cols(jax.random.fold_in(key_of[3], 71), 0)
    return {"blocks": blocks, "block_rows": block_rows, "block_cols": block_cols}


def slot_tables(block_rows, block_cols):
    tile_width = 2 * BROW
    cell_ids = jnp.arange(BROW * tile_width, dtype=jnp.int32)
    cell_code = jnp.where(block_rows >= 0, block_rows * tile_width + block_cols, -1)
    position_index = jnp.arange(SLOTS, dtype=jnp.int32)[:, None]

    def table_of(codes):
        pairing_hits = codes[:, None] == cell_ids[None, :]
        located_position = jnp.sum(jnp.where(pairing_hits, position_index, 0), axis=0).astype(jnp.int32)
        return jnp.where(jnp.any(pairing_hits, axis=0), located_position, SLOTS).reshape(BROW, tile_width)

    return jax.vmap(jax.vmap(table_of))(cell_code)


def reference(blocks, block_rows, block_cols):
    tables = slot_tables(block_rows, block_cols)
    padded = jnp.concatenate([blocks, jnp.zeros((N_ROW, N_COL, 1, BS, BS), blocks.dtype)], axis=2)

    def one_device(device_flat):
        grid_row = device_flat // N_COL
        mesh_across = device_flat % N_COL
        resident_rows = block_rows[grid_row, mesh_across]
        own_cols = block_cols[grid_row, mesh_across]
        row_local = jnp.maximum(resident_rows, 0)
        col_local = jnp.maximum(own_cols, 0)
        summed = jnp.zeros((SLOTS, BS, BS), jnp.float32)
        for step in range(2):
            panel = (grid_row + step) % N_ROW
            left_table = tables[panel, grid_row // 2]
            right_table = tables[panel, mesh_across]
            left_index = left_table[:, (grid_row % 2) * BROW + row_local].T
            right_index = right_table[:, col_local].T
            left_blocks = padded[panel, grid_row // 2][left_index].astype(jnp.float32)
            right_blocks = padded[panel, mesh_across][right_index].astype(jnp.float32)
            summed = summed + jnp.einsum('tkxi,tkxj->tij', left_blocks, right_blocks)
        return jnp.where((resident_rows >= 0)[:, None, None], summed, jnp.float32(0.0)).astype(jnp.bfloat16)

    result = lax.map(one_device, jnp.arange(N_ROW * N_COL, dtype=jnp.int32))
    return result.reshape(N_ROW, N_COL, SLOTS, BS, BS)
```

```python
import functools

import jax
import jax.numpy as jnp
from jax import lax
from jax.experimental import pallas as pl
from jax.experimental.pallas import tpu as pltpu
from jax.sharding import PartitionSpec as P

MESH = pl.DeviceIdType.MESH
BS = 128
BROW = 13
HALF = 20
SLOTS = 40
N_ROW = 32
N_COL = 16
PIECES = 4
PER = HALF // PIECES
PIECE_ROWS = PER * BS + 16
SHIFT_PARTS = 5
SHIFT_SLOTS = SLOTS // SHIFT_PARTS


def gather_kernel(
    rows_s, cols_s, blocks,
    left, shifted, shifted_meta,
    held, stage, meta, order_v, order_s,
    local_sem, root_sem, piece_sem, z_sem, x_sem, core_sem,
    shift_send, shift_recv, meta_send, meta_recv,
):
    r, c = lax.axis_index("row"), lax.axis_index("col")
    zh, x, k = c // 8, (c // 2) % 4, c % 2
    above, below = (r + 1) % N_ROW, (r + N_ROW - 1) % N_ROW
    root_col = r // 2
    primary = zh == root_col // 8
    first_root = c == root_col
    second_root = c == below // 2
    own_first = jnp.logical_and(first_root, k == 0)

    def at(x_of, k_of, zh_of=zh):
        return zh_of * 8 + x_of * 2 + k_of

    ring = [(x + d) % 4 for d in (1, 3, 2)]
    barrier = pltpu.get_barrier_semaphore()

    def greet(row, col):
        pl.semaphore_signal(barrier, inc=1, device_id=(row, col), device_id_type=MESH)

    greet(above, c)
    greet(r, at(x, 1 - k))
    for x_of in ring:
        greet(r, at(x_of, k))

    @pl.when(jnp.logical_not(primary))
    def _():
        greet(r, at(x, k, 1 - zh))

    @pl.when(jnp.logical_and(primary, jnp.logical_and(k == 0, jnp.logical_not(first_root))))
    def _():
        greet(r, root_col)

    @pl.when(jnp.logical_and(primary, k == 1))
    def _():
        greet(above, root_col)

    is_root = jnp.logical_or(first_root, second_root)

    @pl.when(is_root)
    def _():
        pltpu.make_async_copy(blocks, held, local_sem.at[0]).start()

    lane = lax.broadcasted_iota(jnp.int32, (8, 128), 1)
    sub = lax.broadcasted_iota(jnp.int32, (8, 128), 0)

    def place(t, carry):
        n0, n1, own, order, line, column = carry
        a, b = rows_s[t], cols_s[t]
        half = jnp.where(b >= BROW, 1, 0)
        live = jnp.where(a >= 0, 1, 0)
        spot = jnp.where(a >= 0, jnp.where(b >= BROW, n1, n0), 127)
        mine = jnp.logical_and(lane == spot, sub == half)
        own = jnp.where(lane == t, jnp.where(sub == 0, a, b), own)
        order = jnp.where(mine, t, order)
        line = jnp.where(mine, a, line)
        column = jnp.where(mine, b - BROW * half, column)
        return n0 + live * (1 - half), n1 + live * half, own, order, line, column

    zero = jnp.zeros((8, 128), jnp.int32)
    _, _, own, order, line, column = lax.fori_loop(
        0, SLOTS, place, (jnp.int32(0), jnp.int32(0), zero, zero, zero - 1, zero)
    )
    meta[...] = own

    @pl.when(is_root)
    def _():
        order_v[...] = order
        to_scalars = pltpu.make_async_copy(order_v, order_s, local_sem.at[1])
        to_scalars.start()
        pltpu.make_async_copy(blocks, held, local_sem.at[0]).wait()
        to_scalars.wait()

    sub16 = lax.broadcasted_iota(jnp.int32, (16, 128), 0)

    def pack(role, half):
        rows_of = jnp.where(half == 0, line[0:1, :], line[1:2, :])
        cols_of = jnp.where(half == 0, column[0:1, :], column[1:2, :])
        tile = jnp.where(sub16 == 0, rows_of, jnp.where(sub16 == 1, cols_of, 0))
        tile = tile.astype(jnp.float32).astype(jnp.bfloat16)
        for i in range(PIECES):
            for j in range(PER):
                stage[role, i, j * BS:(j + 1) * BS, :] = held[order_s[half, i * PER + j]]
            stage[role, i, PER * BS:, :] = tile

    @pl.when(first_root)
    def _():
        pack(0, r % 2)

    @pl.when(second_root)
    def _():
        pack(1, below % 2)

    def remote(src, dst, send, recv, row, col):
        return pltpu.make_async_remote_copy(
            src_ref=src, dst_ref=dst, send_sem=send, recv_sem=recv, device_id=(row, col), device_id_type=MESH
        )

    def root_copy(role, i, row):
        return remote(
            stage.at[role, i], left.at[role, i], root_sem.at[role, i], piece_sem.at[role, i], row, at(i, role)
        )

    def keep_own():
        return pltpu.make_async_copy(stage.at[0, x], left.at[0, x], local_sem.at[2])

    def shift_copy(i):
        part = pl.ds(i * SHIFT_SLOTS, SHIFT_SLOTS)
        return remote(blocks.at[part], shifted.at[part], shift_send.at[i], shift_recv.at[i], below, c)

    def z_copy():
        return remote(left.at[k, x], left.at[k, x], z_sem.at[0], piece_sem.at[k, x], r, at(x, k, 1 - zh))

    def x_copy(n):
        return remote(left.at[k, x], left.at[k, x], x_sem.at[n], piece_sem.at[k, x], r, at(ring[n], k))

    def core_copy(n, i):
        return remote(left.at[k, i], left.at[k, i], core_sem.at[n], piece_sem.at[k, i], r, at(x, 1 - k))

    def arrived(panel, i):
        remote(left.at[panel, i], left.at[panel, i], core_sem.at[0], piece_sem.at[panel, i], r, at(x, 1 - k)).wait_recv()

    meta_copy = remote(meta, shifted_meta, meta_send.at[0], meta_recv.at[0], below, c)

    sends = (
        5
        + jnp.where(primary, 1, 0)
        + jnp.where(first_root, 4 - jnp.where(k == 0, 1, 0), 0)
        + jnp.where(second_root, 4, 0)
    )
    pl.semaphore_wait(barrier, sends)

    @pl.when(first_root)
    def _():
        for i in range(PIECES):
            @pl.when(jnp.logical_not(jnp.logical_and(own_first, x == i)))
            def _():
                root_copy(0, i, r).start()

    @pl.when(second_root)
    def _():
        for i in range(PIECES):
            root_copy(1, i, below).start()

    @pl.when(own_first)
    def _():
        keep_own().start()

    meta_copy.start()
    for i in range(SHIFT_PARTS):
        shift_copy(i).start()

    @pl.when(own_first)
    def _():
        keep_own().wait()

    @pl.when(jnp.logical_not(own_first))
    def _():
        arrived(k, x)

    @pl.when(primary)
    def _():
        z_copy().start()

    for n in range(3):
        x_copy(n).start()
    core_copy(0, x).start()
    for n in range(3):
        arrived(k, ring[n])
        core_copy(1 + n, ring[n]).start()
    for i in range(PIECES):
        arrived(1 - k, i)

    @pl.when(first_root)
    def _():
        for i in range(PIECES):
            @pl.when(jnp.logical_not(jnp.logical_and(own_first, x == i)))
            def _():
                root_copy(0, i, r).wait_send()

    @pl.when(second_root)
    def _():
        for i in range(PIECES):
            root_copy(1, i, below).wait_send()

    @pl.when(primary)
    def _():
        z_copy().wait_send()

    for n in range(3):
        x_copy(n).wait_send()
    core_copy(0, x).wait_send()
    for n in range(3):
        core_copy(1 + n, ring[n]).wait_send()
    meta_copy.wait()
    for i in range(SHIFT_PARTS):
        shift_copy(i).wait()


def gather(rows, cols, blocks):
    any_space = pl.BlockSpec(memory_space=pl.ANY)
    scalars = pl.BlockSpec(memory_space=pltpu.SMEM)
    dma = pltpu.SemaphoreType.DMA
    return pl.pallas_call(
        gather_kernel,
        name="gather",
        out_shape=(
            jax.ShapeDtypeStruct((2, PIECES, PIECE_ROWS, BS), jnp.bfloat16),
            jax.ShapeDtypeStruct((SLOTS, BS, BS), jnp.bfloat16),
            jax.ShapeDtypeStruct((8, 128), jnp.int32),
        ),
        in_specs=[scalars, scalars, any_space],
        out_specs=(any_space, any_space, any_space),
        scratch_shapes=[
            pltpu.VMEM((SLOTS, BS, BS), jnp.bfloat16),
            pltpu.VMEM((2, PIECES, PIECE_ROWS, BS), jnp.bfloat16),
            pltpu.VMEM((8, 128), jnp.int32),
            pltpu.VMEM((8, 128), jnp.int32),
            pltpu.SMEM((8, 128), jnp.int32),
            dma((3,)),
            dma((2, PIECES)),
            dma((2, PIECES)),
            dma((1,)),
            dma((3,)),
            dma((PIECES,)),
            dma((SHIFT_PARTS,)),
            dma((SHIFT_PARTS,)),
            dma((1,)),
            dma((1,)),
        ],
        compiler_params=pltpu.CompilerParams(
            collective_id=0, has_side_effects=True, vmem_limit_bytes=16 * 1024 * 1024
        ),
    )(rows, cols, blocks)


def multiply_kernel(
    rows_s, cols_s, shifted_s, blocks, shifted, left, out,
    coords_v, coords_s, left_mask, right_mask, left_slot, right_slot, total, sem,
):
    for p in range(2):
        coords_v[p] = left[p, 0, PER * BS:, :].astype(jnp.float32).astype(jnp.int32)
    to_scalars = pltpu.make_async_copy(coords_v, coords_s, sem)
    to_scalars.start()
    out[...] = jnp.zeros_like(out)

    @pl.loop(0, 32)
    def _(i):
        left_mask[i] = 0
        right_mask[i] = 0
        right_mask[i + 32] = 0

    def add_right(p, a, b, t):
        @pl.when(a >= 0)
        def _():
            right_mask[p * 32 + b] = right_mask[p * 32 + b] | (1 << a)
            right_slot[p * 512 + b * 16 + a] = t

    @pl.loop(0, SLOTS)
    def _(t):
        add_right(0, rows_s[t], cols_s[t], t)
        add_right(1, shifted_s[0, t], shifted_s[1, t], t)

    to_scalars.wait()

    @pl.loop(0, HALF)
    def _(j):
        for p in range(2):
            a, b = coords_s[p, 0, j], coords_s[p, 1, j]

            @pl.when(a >= 0)
            def _():
                left_mask[p * 16 + b] = left_mask[p * 16 + b] | (1 << a)
                left_slot[p * 256 + b * 16 + a] = j

    @pl.loop(0, SLOTS)
    def _(t):
        a, b = rows_s[t], cols_s[t]

        @pl.when(a >= 0)
        def _():
            meet = [left_mask[p * 16 + a] & right_mask[p * 32 + b] for p in range(2)]

            @pl.when((meet[0] | meet[1]) != 0)
            def _():
                total[...] = jnp.zeros_like(total)
                for p, right in enumerate((blocks, shifted)):
                    @pl.when(meet[p] != 0)
                    def _():
                        @pl.loop(0, BROW)
                        def _(m):
                            @pl.when(((meet[p] >> m) & 1) != 0)
                            def _():
                                j = left_slot[p * 256 + a * 16 + m]
                                piece = j // PER
                                start = pl.multiple_of((j - piece * PER) * BS, BS)
                                total[...] += lax.dot_general(
                                    left[p, piece, pl.ds(start, BS), :],
                                    right[right_slot[p * 512 + b * 16 + m]],
                                    (((0,), (0,)), ((), ())),
                                    preferred_element_type=jnp.float32,
                                )
                out[t] = total[...].astype(jnp.bfloat16)


def multiply(rows, cols, shifted_meta, blocks, shifted, left):
    scalars = pl.BlockSpec(memory_space=pltpu.SMEM)
    vectors = pl.BlockSpec(memory_space=pltpu.VMEM)
    return pl.pallas_call(
        multiply_kernel,
        name="multiply",
        out_shape=jax.ShapeDtypeStruct((SLOTS, BS, BS), jnp.bfloat16),
        in_specs=[scalars, scalars, scalars, vectors, vectors, vectors],
        out_specs=vectors,
        scratch_shapes=[
            pltpu.VMEM((2, 16, 128), jnp.int32),
            pltpu.SMEM((2, 16, 128), jnp.int32),
            pltpu.SMEM((32,), jnp.int32),
            pltpu.SMEM((64,), jnp.int32),
            pltpu.SMEM((512,), jnp.int32),
            pltpu.SMEM((1024,), jnp.int32),
            pltpu.VMEM((BS, BS), jnp.float32),
            pltpu.SemaphoreType.DMA,
        ],
        compiler_params=pltpu.CompilerParams(vmem_limit_bytes=32 * 1024 * 1024),
    )(rows, cols, shifted_meta, blocks, shifted, left)


def shards(blocks, block_rows, block_cols):
    blocks, rows, cols = blocks[0, 0], block_rows[0, 0], block_cols[0, 0]
    left, shifted, shifted_meta = gather(rows, cols, blocks)
    product = multiply(rows, cols, shifted_meta, blocks, shifted, left)
    return product[None, None]


def solution(mesh):
    return jax.shard_map(
        shards,
        mesh=mesh,
        in_specs=(P("row", "col", None, None, None), P("row", "col", None), P("row", "col", None)),
        out_specs=P("row", "col", None, None, None),
        check_vma=False,
    )
```

```python
import functools

import jax
import jax.numpy as jnp
from jax import lax
from jax.experimental import pallas as pl
from jax.experimental.pallas import tpu as pltpu
from jax.sharding import PartitionSpec as P

MESH = pl.DeviceIdType.MESH
BS = 128
BROW = 13
HALF = 20
SLOTS = 40
ROOM = 16
N_ROW = 32
N_COL = 16
PIECES = 4
PER = HALF // PIECES
PIECE_ROWS = PER * BS
CHUNKS = ((0, 320), (320, PIECE_ROWS))
ASIDE = (0,)
STRAIGHT = (1,)
ORDER = (1, 0)
MEETINGS = 2 * 178
GROUP = 4


def gather_kernel(
    partial,
    rows_s, cols_s, blocks,
    left, right, metas, flag,
    held, stage, packed, meta, below_meta, root_meta, order_v, order_s, need_v, need_s, onward, aside,
    chip_flags, z_flags, y_flags, flag_v,
    local_sem, root_sem, piece_sem, onward_sem, aside_sem, cross_sem, near_sem, x_sem, core_sem,
    shift_send, shift_recv, meta_send, meta_recv, flag_send, flag_recv,
):
    r, c = lax.axis_index("row"), lax.axis_index("col")
    y, zl = r // 8, r % 8
    zh, x, k = c // 8, (c // 2) % 4, c % 2
    z = zh * 8 + zl
    above, below = (r + 1) % N_ROW, (r + N_ROW - 1) % N_ROW

    def mirrored(row):
        return row + 8 * (3 - 2 * (row // 8))

    def home(row):
        return row // 16

    across = mirrored(r)
    across_below = (across + N_ROW - 1) % N_ROW
    first_root = c == r // 2
    second_root = c == below // 2
    first_panel, second_panel = k == 0, k == 1
    own_first = jnp.logical_and(first_root, first_panel)
    own_second = jnp.logical_and(second_root, second_panel)
    near = zh == home(r)
    far = jnp.logical_not(near)
    near_first = jnp.logical_and(first_panel, near)
    aside_first = jnp.logical_and(first_panel, far)
    near_second = jnp.logical_and(second_panel, zh == home(below))
    aside_second = jnp.logical_and(second_panel, zh == home(across_below))

    def at(x_of, k_of, zh_of=zh):
        return zh_of * 8 + x_of * 2 + k_of

    same, other = at(x, k), at(x, k, 1 - zh)
    ring = [(x + d) % 4 for d in (1, 3, 2)]
    chip_peers = [(r, zh * 8 + (x * 2 + k + d) % 8) for d in range(1, 8)]
    z_peers = [(y * 8 + (z + d) % 8, ((z + d) % 16) // 8 * 8 + x * 2 + k) for d in range(1, 16)]
    y_peers = [((y + d) % 4 * 8 + zl, c) for d in range(1, 4)]
    row_peers = [(r, (c + d) % N_COL) for d in range(1, N_COL)]
    barrier = pltpu.get_barrier_semaphore()

    def greet(row, col):
        pl.semaphore_signal(barrier, inc=1, device_id=(row, col), device_id_type=MESH)

    def greet_if(condition, row, col):
        @pl.when(condition)
        def _():
            greet(row, col)

    greet_if(jnp.logical_and(first_panel, far), r, other)
    greet_if(jnp.logical_and(first_panel, far), across, other)
    greet_if(jnp.logical_and(second_panel, far), above, other)
    greet_if(jnp.logical_and(second_panel, far), mirrored(above), other)
    greet(above, r // 2)
    greet_if(jnp.logical_not(first_root), r, r // 2)
    greet_if(jnp.logical_and(second_panel, near), above, same)
    greet(above, c)
    greet_if(jnp.logical_and(near_first, jnp.logical_not(own_first)), r, r // 2)
    greet_if(aside_first, across, across // 2)
    greet_if(jnp.logical_and(near_second, jnp.logical_not(own_second)), r, below // 2)
    greet_if(aside_second, across, across_below // 2)
    if partial:
        greet_if(jnp.logical_not(second_root), r, below // 2)
        greet(below, c)
        for peer in z_peers + y_peers + chip_peers:
            greet(*peer)
    greet(r, at(x, 1 - k))
    for x_of in ring:
        greet(r, at(x_of, k))

    is_root = jnp.logical_or(first_root, second_root)

    def fetch():
        return pltpu.make_async_copy(blocks, held, local_sem.at[0])

    if partial:
        fetch().start()
    else:
        pl.when(is_root)(lambda: fetch().start())

    lane = lax.broadcasted_iota(jnp.int32, (8, 128), 1)
    sub = lax.broadcasted_iota(jnp.int32, (8, 128), 0)

    def place(t, carry):
        n0, n1, own, order = carry
        a, b = rows_s[t], cols_s[t]
        half = jnp.where(b >= BROW, 1, 0)
        live = jnp.where(a >= 0, 1, 0)
        spot = jnp.where(a >= 0, jnp.where(b >= BROW, n1, n0), 127)
        own = jnp.where(lane == t, jnp.where(sub == 0, a, b), own)
        order = jnp.where(jnp.logical_and(lane == spot, sub == half), t, order)
        return n0 + live * (1 - half), n1 + live * half, own, order

    zero = jnp.zeros((8, 128), jnp.int32)
    _, _, own, order = lax.fori_loop(0, SLOTS, place, (jnp.int32(0), jnp.int32(0), zero - 1, zero))
    meta[...] = own

    @pl.when(is_root)
    def _():
        order_v[...] = order
        to_scalars = pltpu.make_async_copy(order_v, order_s, local_sem.at[1])
        to_scalars.start()
        to_scalars.wait()

    if partial:
        fetch().wait()
    else:
        pl.when(is_root)(lambda: fetch().wait())

    def pack(role, half):
        for i in range(PIECES):
            for j in range(PER):
                stage[role, i, j * BS:(j + 1) * BS, :] = held[jnp.clip(order_s[half, i * PER + j], 0, SLOTS - 1)].T

    @pl.when(first_root)
    def _():
        pack(0, r % 2)

    @pl.when(second_root)
    def _():
        pack(1, below % 2)

    def remote(src, dst, send, recv, row, col):
        return pltpu.make_async_remote_copy(
            src_ref=src, dst_ref=dst, send_sem=send, recv_sem=recv, device_id=(row, col), device_id_type=MESH
        )

    def chunk(ref, h):
        first, last = CHUNKS[h]
        return ref.at[pl.ds(first, last - first)]

    def pass_on(panel, i, h, send, row, col, source=None):
        here = chunk(left.at[panel, i], h)
        return remote(here if source is None else source, here, send, piece_sem.at[panel, i, h], row, col)

    def first_copy(i, h):
        return pass_on(0, i, h, root_sem.at[0, 0, i, h], r, at(i, 0), chunk(stage.at[0, i], h))

    def second_copy(i, h):
        return remote(
            chunk(stage.at[1, i], h), chunk(onward, h), root_sem.at[1, 0, i, h], onward_sem.at[h], r, at(i, 1)
        )

    def aside_copy(role, i, h):
        return remote(
            chunk(stage.at[role, i], h), chunk(aside, h), root_sem.at[role, 1, i, h], aside_sem.at[h], across, at(i, role)
        )

    def for_root_copies(do):
        def both(role, i, h, direct, own):
            if h in ASIDE:
                do(aside_copy(role, i, h))

            @pl.when(jnp.logical_not(jnp.logical_and(own, x == i)))
            def _():
                do(direct(i, h))

        @pl.when(first_root)
        def _():
            for h in ORDER:
                for i in range(PIECES):
                    both(0, i, h, first_copy, own_first)

        @pl.when(second_root)
        def _():
            for h in ORDER:
                for i in range(PIECES):
                    both(1, i, h, second_copy, own_second)

    def keep(condition, source, target, do):
        @pl.when(condition)
        def _():
            do(pltpu.make_async_copy(source, target, local_sem.at[2]))

    def keep_first(do):
        keep(own_first, stage.at[0, x], left.at[0, x], do)

    def keep_second(do):
        keep(own_second, stage.at[1, x], onward, do)

    def first_meta(peer):
        return remote(meta, metas.at[0], meta_send.at[0], meta_recv.at[0], *peer)

    def second_meta(peer):
        return remote(meta, metas.at[1], meta_send.at[1], meta_recv.at[1], *peer)

    def home_meta(peer):
        return remote(meta, root_meta, meta_send.at[4], meta_recv.at[4], *peer)

    shift_meta = remote(meta, metas.at[2], meta_send.at[2], meta_recv.at[2], below, c)
    if partial:
        upward_meta = remote(meta, below_meta, meta_send.at[3], meta_recv.at[3], above, c)

    def sent(n, send):
        many = z_flags.at[pl.ds(0, n)]
        remote(many, many, send, flag_recv.at[0], below, c).wait_send()

    slots = ROOM if partial else SLOTS
    parts = 2 if partial else 5

    def shift_copy(i):
        part = pl.ds(i * (slots // parts), slots // parts)
        source = packed if partial else blocks
        return remote(source.at[part], right.at[part], shift_send.at[i], shift_recv.at[i], below, c)

    def straight_first(h):
        return pass_on(0, x, h, cross_sem.at[h], r, other)

    def straight_second(h):
        return pass_on(1, x, h, cross_sem.at[h], below, other, chunk(onward, h))

    def to_near(h):
        return pass_on(1, x, h, near_sem.at[h], below, same, chunk(onward, h))

    def from_aside(role, h):
        return pass_on(role, x, h, cross_sem.at[h], across if role == 0 else across_below, other, chunk(aside, h))

    def x_copy(n, h):
        return pass_on(k, x, h, x_sem.at[n, h], r, at(ring[n], k))

    def core_copy(n, i, h):
        return pass_on(k, i, h, core_sem.at[n, h], r, at(x, 1 - k))

    def arrived(panel, i, h):
        pass_on(panel, i, h, core_sem.at[0, 0], r, at(x, 1 - k)).wait_recv()

    def landed(ref, h, sem):
        remote(chunk(ref, h), chunk(ref, h), core_sem.at[0, 0], sem.at[h], r, at(x, 1 - k)).wait_recv()

    def amount(condition, n):
        return jnp.where(condition, n, 0)

    sends = (
        5
        + amount(first_root, 8 + 15) - amount(own_first, 1)
        + amount(second_root, 8 + 16) - amount(own_second, 1)
        + amount(near_first, 1) + amount(aside_first, 1) + amount(near_second, 2) + amount(aside_second, 1)
    )
    if partial:
        sends = sends + 1 + 25 + amount(second_root, 15)
    pl.semaphore_wait(barrier, sends)

    if partial:
        upward_meta.start()

        @pl.when(second_root)
        def _():
            for peer in row_peers:
                home_meta(peer).start()
            root_meta[...] = meta[...]

    for_root_copies(lambda copy: copy.start())
    keep_first(lambda copy: copy.start())
    keep_second(lambda copy: copy.start())
    shift_meta.start()

    if not partial:
        for i in range(parts):
            shift_copy(i).start()

    def own_meta():
        return pltpu.make_async_copy(meta, metas.at[0], local_sem.at[1])

    @pl.when(first_root)
    def _():
        for peer in row_peers:
            first_meta(peer).start()
        own_meta().start()

    @pl.when(second_root)
    def _():
        for col in range(N_COL):
            second_meta((below, col)).start()

    keep_first(lambda copy: copy.wait())
    keep_second(lambda copy: copy.wait())

    def spread(h):
        for n in range(3):
            x_copy(n, h).start()
        core_copy(0, x, h).start()

    @pl.when(near_first)
    def _():
        for h in ORDER:
            @pl.when(jnp.logical_not(own_first))
            def _():
                arrived(0, x, h)

            if h in STRAIGHT:
                straight_first(h).start()
            spread(h)

    @pl.when(aside_first)
    def _():
        for h in ASIDE:
            landed(aside, h, aside_sem)
            from_aside(0, h).start()

    @pl.when(near_second)
    def _():
        for h in ORDER:
            @pl.when(jnp.logical_not(own_second))
            def _():
                landed(onward, h, onward_sem)

            if h in STRAIGHT:
                straight_second(h).start()
            to_near(h).start()

    @pl.when(aside_second)
    def _():
        for h in ASIDE:
            landed(aside, h, aside_sem)
            from_aside(1, h).start()

    def send_flags(peers, buffer, me, n):
        buffer[me] = flag_v[n]
        for peer in peers:
            remote(flag_v.at[n], buffer.at[me], flag_send.at[n], flag_recv.at[n], *peer).start()

    def join_flags(buffer, count, n):
        others = buffer.at[pl.ds(0, count - 1)]
        remote(others, others, flag_send.at[n], flag_recv.at[n], below, c).wait_recv()
        joined = buffer[0]
        for i in range(1, count):
            joined = jnp.maximum(joined, buffer[i])
        return joined

    if partial:
        upward_meta.wait_recv()

        @pl.when(jnp.logical_not(second_root))
        def _():
            home_meta(row_peers[0]).wait_recv()

        wide_lane = lax.broadcasted_iota(jnp.int32, (SLOTS, 128), 1)
        wide_sub = lax.broadcasted_iota(jnp.int32, (SLOTS, 128), 0)

        def down(values):
            return jnp.sum(jnp.where(wide_lane == wide_sub, values, 0), axis=1, keepdims=True)

        def bits(rows, valid):
            return jnp.where(valid, jnp.left_shift(1, jnp.maximum(rows, 0)), 0)

        def union(keys, masks, wanted):
            return jnp.sum(jnp.where(down(keys) == wanted, down(masks), 0), axis=0, keepdims=True)

        line, column = own[0:1, :], own[1:2, :]
        theirs, half_meta = below_meta[...], root_meta[...]
        left_line, left_column = half_meta[0:1, :], half_meta[1:2, :] - BROW * (below % 2)
        in_half = jnp.logical_and(left_line >= 0, jnp.logical_and(left_column >= 0, left_column < BROW))
        by_line = union(left_line, bits(jnp.minimum(left_column, BROW), in_half), line)
        by_column = union(theirs[1:2, :], bits(theirs[0:1, :], theirs[0:1, :] >= 0), column)
        needed = jnp.logical_and(line >= 0, jnp.bitwise_and(by_line, by_column) != 0)
        count = jnp.where(needed, 1, 0)
        rank = jnp.sum(jnp.where(wide_sub < wide_lane, down(count), 0), axis=0, keepdims=True)
        spot_sub = lax.broadcasted_iota(jnp.int32, (ROOM, 128), 0)
        spot_lane = lax.broadcasted_iota(jnp.int32, (ROOM, 128), 1)
        chosen = jnp.logical_and(needed, rank == spot_sub)
        slot = jnp.sum(jnp.where(chosen, spot_lane, 0), axis=1, keepdims=True)
        need_v[...] = jnp.broadcast_to(slot, (ROOM, 128))
        needs = pltpu.make_async_copy(need_v, need_s, local_sem.at[3])
        needs.start()
        total = jnp.sum(count, axis=1, keepdims=True)
        flag_v[0] = jnp.broadcast_to(jnp.where(total > ROOM, 1, 0), (8, 128))
        needs.wait()
        for s in range(ROOM):
            packed[s] = held[jnp.clip(need_s[s, 0], 0, SLOTS - 1)]
        for i in range(parts):
            shift_copy(i).start()
        send_flags(chip_peers, chip_flags, x * 2 + k, 0)

    if partial:
        flag_v[1] = join_flags(chip_flags, 8, 0)
        send_flags(z_peers, z_flags, z, 1)

    @pl.when(jnp.logical_not(near_first))
    def _():
        for h in ORDER:
            arrived(k, x, h)
            spread(h)

    if partial:
        flag_v[2] = join_flags(z_flags, 16, 1)
        send_flags(y_peers, y_flags, y, 2)

    for h in ORDER:
        for n in range(3):
            arrived(k, ring[n], h)
            core_copy(1 + n, ring[n], h).start()

    for h in ORDER:
        for i in range(PIECES):
            arrived(1 - k, i, h)

    if partial:
        flag[0, 0] = jnp.max(join_flags(y_flags, 4, 2))
        sent(7, flag_send.at[0])
        sent(15, flag_send.at[1])
        sent(3, flag_send.at[2])
    else:
        flag[0, 0] = 0

    for_root_copies(lambda copy: copy.wait_send())

    @pl.when(first_root)
    def _():
        own_meta().wait()
        sent(15, meta_send.at[0])

    @pl.when(jnp.logical_not(first_root))
    def _():
        first_meta(row_peers[0]).wait_recv()

    @pl.when(second_root)
    def _():
        sent(16, meta_send.at[1])

    second_meta((below, c)).wait_recv()
    shift_meta.wait()
    if partial:
        upward_meta.wait_send()

        @pl.when(second_root)
        def _():
            sent(15, meta_send.at[4])

    @pl.when(near_first)
    def _():
        for h in STRAIGHT:
            straight_first(h).wait_send()

    @pl.when(near_second)
    def _():
        for h in STRAIGHT:
            straight_second(h).wait_send()
        for h in ORDER:
            to_near(h).wait_send()

    @pl.when(aside_first)
    def _():
        for h in ASIDE:
            from_aside(0, h).wait_send()

    @pl.when(aside_second)
    def _():
        for h in ASIDE:
            from_aside(1, h).wait_send()

    for h in ORDER:
        for n in range(3):
            x_copy(n, h).wait_send()
        core_copy(0, x, h).wait_send()
        for n in range(3):
            core_copy(1 + n, ring[n], h).wait_send()
    for i in range(parts):
        shift_copy(i).wait()


def gather(rows, cols, blocks, partial):
    any_space = pl.BlockSpec(memory_space=pl.ANY)
    scalars = pl.BlockSpec(memory_space=pltpu.SMEM)
    dma = pltpu.SemaphoreType.DMA
    tile = (8, 128)
    hops = len(CHUNKS)
    return pl.pallas_call(
        functools.partial(gather_kernel, partial),
        name="gather_needed" if partial else "gather_all",
        out_shape=(
            jax.ShapeDtypeStruct((2, PIECES, PIECE_ROWS, BS), jnp.bfloat16),
            jax.ShapeDtypeStruct((ROOM if partial else SLOTS, BS, BS), jnp.bfloat16),
            jax.ShapeDtypeStruct((3, *tile), jnp.int32),
            jax.ShapeDtypeStruct((1, 1), jnp.int32),
        ),
        in_specs=[scalars, scalars, any_space],
        out_specs=(any_space, any_space, any_space, scalars),
        scratch_shapes=[
            pltpu.VMEM((SLOTS, BS, BS), jnp.bfloat16),
            pltpu.VMEM((2, PIECES, PIECE_ROWS, BS), jnp.bfloat16),
            pltpu.VMEM((ROOM, BS, BS), jnp.bfloat16),
            pltpu.VMEM(tile, jnp.int32),
            pltpu.VMEM(tile, jnp.int32),
            pltpu.VMEM(tile, jnp.int32),
            pltpu.VMEM(tile, jnp.int32),
            pltpu.SMEM(tile, jnp.int32),
            pltpu.VMEM((ROOM, 128), jnp.int32),
            pltpu.SMEM((ROOM, 128), jnp.int32),
            pltpu.VMEM((PIECE_ROWS, BS), jnp.bfloat16),
            pltpu.VMEM((PIECE_ROWS, BS), jnp.bfloat16),
            pltpu.VMEM((8, *tile), jnp.int32),
            pltpu.VMEM((16, *tile), jnp.int32),
            pltpu.VMEM((4, *tile), jnp.int32),
            pltpu.VMEM((3, *tile), jnp.int32),
            dma((4,)),
            dma((2, 2, PIECES, hops)),
            dma((2, PIECES, hops)),
            dma((hops,)),
            dma((hops,)),
            dma((hops,)),
            dma((hops,)),
            dma((3, hops)),
            dma((PIECES, hops)),
            dma((5,)),
            dma((5,)),
            dma((5,)),
            dma((5,)),
            dma((3,)),
            dma((3,)),
        ],
        compiler_params=pltpu.CompilerParams(
            collective_id=0 if partial else 1, has_side_effects=True, vmem_limit_bytes=GATHER_MIB * 1024 * 1024
        ),
    )(rows, cols, blocks)


GATHER_MIB = 62
MULTIPLY_MIB = 62


def multiply_kernel(
    partial,
    rows_s, cols_s, metas_s, blocks, right, left, out,
    left_mask, right_mask, line_mask, left_slot, right_slot, where_s, slot_s, count_s,
    zeros, left_v, right_v, total, done, zero_sem, load_sem, store_sem,
):
    half = lax.axis_index("row") % 2
    zeros[...] = jnp.zeros_like(zeros)
    clear = pltpu.make_async_copy(zeros, out, zero_sem)
    clear.start()
    for i in range(16):
        line_mask[i] = 0
    for i in range(32):
        left_mask[i] = 0
    for i in range(64):
        right_mask[i] = 0
    count_s[0] = 0
    count_s[1] = 0

    def put(mask, key, live, bit):
        mask[key] = mask[key] | jnp.where(live, jnp.left_shift(1, jnp.maximum(bit, 0)), 0)

    def tables(t, carry):
        found = list(carry)
        a, b = rows_s[t], cols_s[t]
        live = a >= 0
        put(right_mask, jnp.where(live, b, 31), live, a)
        right_slot[jnp.where(live, b * 16 + a, 511)] = t
        for p in range(2):
            m, i = metas_s[p, 0, t], metas_s[p, 1, t] - BROW * half
            live = jnp.logical_and(m >= 0, jnp.logical_and(i >= 0, i < BROW))
            put(left_mask, jnp.where(live, p * 16 + i, 15), live, m)
            left_slot[jnp.where(live, p * 256 + i * 16 + m, 255)] = found[p]
            found[p] = found[p] + jnp.where(live, 1, 0)
            if p == 1:
                put(line_mask, jnp.where(live, m, 15), live, i)
        return tuple(found)

    lax.fori_loop(0, SLOTS, tables, (jnp.int32(0), jnp.int32(0)))

    def second_table(t, found):
        m, b = metas_s[2, 0, t], metas_s[2, 1, t]
        live = m >= 0
        if partial:
            live = jnp.logical_and(live, (line_mask[jnp.where(live, m, 15)] & right_mask[jnp.where(live, b, 31)]) != 0)
            live = jnp.logical_and(live, found < ROOM)
        put(right_mask, jnp.where(live, 32 + b, 63), live, m)
        right_slot[jnp.where(live, 512 + b * 16 + m, 1023)] = found if partial else t
        return found + jnp.where(live, 1, 0)

    lax.fori_loop(0, SLOTS, second_table, jnp.int32(0))

    def load(p, i, m, b, t):
        n = jnp.minimum(count_s[0], MEETINGS - 1)
        j = jnp.minimum(left_slot[p * 256 + i * 16 + m], HALF - 1)
        piece = j // PER
        start = pl.multiple_of((j - piece * PER) * BS, BS)
        source = (blocks, right)[p]
        pltpu.make_async_copy(left.at[p, piece, pl.ds(start, BS)], left_v.at[n], load_sem.at[0]).start()
        slot = jnp.minimum(right_slot[p * 512 + b * 16 + m], source.shape[0] - 1)
        pltpu.make_async_copy(source.at[slot], right_v.at[n], load_sem.at[1]).start()
        where_s[n] = t
        count_s[0] = n + 1

    @pl.loop(0, SLOTS)
    def _(t):
        a, b = rows_s[t], cols_s[t]

        @pl.when(a >= 0)
        def _():
            meet = [left_mask[p * 16 + a] & right_mask[p * 32 + b] for p in range(2)]

            @pl.when((meet[0] | meet[1]) != 0)
            def _():
                slot_s[count_s[1]] = t
                count_s[1] = count_s[1] + 1
                total[t] = jnp.zeros_like(total[t])
                for p in range(2):
                    @pl.when(meet[p] != 0)
                    def _():
                        @pl.loop(0, BROW)
                        def _(m):
                            @pl.when(((meet[p] >> m) & 1) != 0)
                            def _():
                                load(p, a, m, b, t)

    n, slots = count_s[0], count_s[1]
    for u in range(GROUP):
        where_s[n + u] = SLOTS

    @pl.loop(0, n)
    def _(i):
        pltpu.make_async_copy(blocks.at[0], left_v.at[0], load_sem.at[0]).wait()
        pltpu.make_async_copy(blocks.at[0], right_v.at[0], load_sem.at[1]).wait()

    @pl.loop(0, (n + GROUP - 1) // GROUP)
    def _(g):
        products = [
            jnp.dot(left_v[g * GROUP + u], right_v[g * GROUP + u], preferred_element_type=jnp.float32)
            for u in range(GROUP)
        ]
        for u in range(GROUP):
            t = where_s[g * GROUP + u]
            total[t] = total[t] + products[u]

    clear.wait()

    @pl.loop(0, slots)
    def _(i):
        t = slot_s[i]
        done[i] = total[t].astype(jnp.bfloat16)
        pltpu.make_async_copy(done.at[i], out.at[t], store_sem).start()

    @pl.loop(0, slots)
    def _(i):
        pltpu.make_async_copy(done.at[0], out.at[0], store_sem).wait()


def multiply(rows, cols, metas, blocks, right, left, partial):
    scalars = pl.BlockSpec(memory_space=pltpu.SMEM)
    any_space = pl.BlockSpec(memory_space=pl.ANY)
    room = MEETINGS + GROUP
    return pl.pallas_call(
        functools.partial(multiply_kernel, partial),
        name="multiply",
        out_shape=jax.ShapeDtypeStruct((SLOTS, BS, BS), jnp.bfloat16),
        in_specs=[scalars, scalars, scalars, any_space, any_space, any_space],
        out_specs=any_space,
        scratch_shapes=[
            pltpu.SMEM((32,), jnp.int32),
            pltpu.SMEM((64,), jnp.int32),
            pltpu.SMEM((16,), jnp.int32),
            pltpu.SMEM((512,), jnp.int32),
            pltpu.SMEM((1024,), jnp.int32),
            pltpu.SMEM((room,), jnp.int32),
            pltpu.SMEM((SLOTS,), jnp.int32),
            pltpu.SMEM((2,), jnp.int32),
            pltpu.VMEM((SLOTS, BS, BS), jnp.bfloat16),
            pltpu.VMEM((room, BS, BS), jnp.bfloat16),
            pltpu.VMEM((room, BS, BS), jnp.bfloat16),
            pltpu.VMEM((SLOTS + 1, BS, BS), jnp.float32),
            pltpu.VMEM((SLOTS, BS, BS), jnp.bfloat16),
            pltpu.SemaphoreType.DMA,
            pltpu.SemaphoreType.DMA((2,)),
            pltpu.SemaphoreType.DMA,
        ],
        compiler_params=pltpu.CompilerParams(vmem_limit_bytes=MULTIPLY_MIB * 1024 * 1024),
    )(rows, cols, metas, blocks, right, left)


def product(rows, cols, blocks, partial):
    left, right, metas, flag = gather(rows, cols, blocks, partial)
    return multiply(rows, cols, metas, blocks, right, left, partial), flag


def shards(blocks, block_rows, block_cols):
    blocks, rows, cols = blocks[0, 0], block_rows[0, 0], block_cols[0, 0]
    result, flag = product(rows, cols, blocks, True)
    result = lax.cond(flag[0, 0] > 0, lambda: product(rows, cols, blocks, False)[0], lambda: result)
    return result[None, None]


def solution(mesh):
    return jax.shard_map(
        shards,
        mesh=mesh,
        in_specs=(P("row", "col", None, None, None), P("row", "col", None), P("row", "col", None)),
        out_specs=P("row", "col", None, None, None),
        check_vma=False,
    )
```

```python
import functools

import jax
import jax.numpy as jnp
from jax import lax
from jax.experimental import pallas as pl
from jax.experimental.pallas import tpu as pltpu
from jax.sharding import PartitionSpec as P

MESH = pl.DeviceIdType.MESH
BS = 128
BROW = 13
HALF = 20
SLOTS = 40
ROOM = 16
N_ROW = 32
N_COL = 16
PIECES = 4
PER = HALF // PIECES
PIECE_ROWS = PER * BS
CHUNKS = ((0, 320), (320, PIECE_ROWS))
ASIDE = (0,)
STRAIGHT = (1,)
ORDER = (1, 0)
MEETINGS = 2 * 178
GROUP = 4


def gather_kernel(
    partial,
    rows_s, cols_s, blocks,
    left, right, plan, flag,
    metas, held, stage, packed, meta, below_meta, root_meta, order_v, order_s, need_v, need_s, onward, aside,
    chip_flags, z_flags, y_flags, flag_v,
    local_sem, root_sem, piece_sem, onward_sem, aside_sem, cross_sem, near_sem, x_sem, core_sem,
    shift_send, shift_recv, meta_send, meta_recv, flag_send, flag_recv,
):
    r, c = lax.axis_index("row"), lax.axis_index("col")
    y, zl = r // 8, r % 8
    zh, x, k = c // 8, (c // 2) % 4, c % 2
    z = zh * 8 + zl
    above, below = (r + 1) % N_ROW, (r + N_ROW - 1) % N_ROW

    def mirrored(row):
        return row + 8 * (3 - 2 * (row // 8))

    def home(row):
        return row // 16

    across = mirrored(r)
    across_below = (across + N_ROW - 1) % N_ROW
    first_root = c == r // 2
    second_root = c == below // 2
    first_panel, second_panel = k == 0, k == 1
    own_first = jnp.logical_and(first_root, first_panel)
    own_second = jnp.logical_and(second_root, second_panel)
    near = zh == home(r)
    far = jnp.logical_not(near)
    near_first = jnp.logical_and(first_panel, near)
    aside_first = jnp.logical_and(first_panel, far)
    near_second = jnp.logical_and(second_panel, zh == home(below))
    aside_second = jnp.logical_and(second_panel, zh == home(across_below))

    def at(x_of, k_of, zh_of=zh):
        return zh_of * 8 + x_of * 2 + k_of

    same, other = at(x, k), at(x, k, 1 - zh)
    ring = [(x + d) % 4 for d in (1, 3, 2)]
    chip_peers = [(r, zh * 8 + (x * 2 + k + d) % 8) for d in range(1, 8)]
    z_peers = [(y * 8 + (z + d) % 8, ((z + d) % 16) // 8 * 8 + x * 2 + k) for d in range(1, 16)]
    y_peers = [((y + d) % 4 * 8 + zl, c) for d in range(1, 4)]
    row_peers = [(r, (c + d) % N_COL) for d in range(1, N_COL)]
    barrier = pltpu.get_barrier_semaphore()

    def greet(row, col):
        pl.semaphore_signal(barrier, inc=1, device_id=(row, col), device_id_type=MESH)

    def greet_if(condition, row, col):
        @pl.when(condition)
        def _():
            greet(row, col)

    greet_if(jnp.logical_and(first_panel, far), r, other)
    greet_if(jnp.logical_and(first_panel, far), across, other)
    greet_if(jnp.logical_and(second_panel, far), above, other)
    greet_if(jnp.logical_and(second_panel, far), mirrored(above), other)
    greet(above, r // 2)
    greet_if(jnp.logical_not(first_root), r, r // 2)
    greet_if(jnp.logical_and(second_panel, near), above, same)
    greet(above, c)
    greet_if(jnp.logical_and(near_first, jnp.logical_not(own_first)), r, r // 2)
    greet_if(aside_first, across, across // 2)
    greet_if(jnp.logical_and(near_second, jnp.logical_not(own_second)), r, below // 2)
    greet_if(aside_second, across, across_below // 2)
    if partial:
        greet_if(jnp.logical_not(second_root), r, below // 2)
        greet(below, c)
        for peer in z_peers + y_peers + chip_peers:
            greet(*peer)
    greet(r, at(x, 1 - k))
    for x_of in ring:
        greet(r, at(x_of, k))

    is_root = jnp.logical_or(first_root, second_root)

    def fetch():
        return pltpu.make_async_copy(blocks, held, local_sem.at[0])

    if partial:
        fetch().start()
    else:
        pl.when(is_root)(lambda: fetch().start())

    lane = lax.broadcasted_iota(jnp.int32, (8, 128), 1)
    sub = lax.broadcasted_iota(jnp.int32, (8, 128), 0)

    def place(t, carry):
        n0, n1, own, order = carry
        a, b = rows_s[t], cols_s[t]
        half = jnp.where(b >= BROW, 1, 0)
        live = jnp.where(a >= 0, 1, 0)
        spot = jnp.where(a >= 0, jnp.where(b >= BROW, n1, n0), 127)
        own = jnp.where(lane == t, jnp.where(sub == 0, a, b), own)
        order = jnp.where(jnp.logical_and(lane == spot, sub == half), t, order)
        return n0 + live * (1 - half), n1 + live * half, own, order

    zero = jnp.zeros((8, 128), jnp.int32)
    _, _, own, order = lax.fori_loop(0, SLOTS, place, (jnp.int32(0), jnp.int32(0), zero - 1, zero))
    meta[...] = own

    @pl.when(is_root)
    def _():
        order_v[...] = order
        to_scalars = pltpu.make_async_copy(order_v, order_s, local_sem.at[1])
        to_scalars.start()
        to_scalars.wait()

    if partial:
        fetch().wait()
    else:
        pl.when(is_root)(lambda: fetch().wait())

    def pack(role, half):
        for i in range(PIECES):
            for j in range(PER):
                stage[role, i, j * BS:(j + 1) * BS, :] = held[jnp.clip(order_s[half, i * PER + j], 0, SLOTS - 1)].T

    @pl.when(first_root)
    def _():
        pack(0, r % 2)

    @pl.when(second_root)
    def _():
        pack(1, below % 2)

    def remote(src, dst, send, recv, row, col):
        return pltpu.make_async_remote_copy(
            src_ref=src, dst_ref=dst, send_sem=send, recv_sem=recv, device_id=(row, col), device_id_type=MESH
        )

    def chunk(ref, h):
        first, last = CHUNKS[h]
        return ref.at[pl.ds(first, last - first)]

    def pass_on(panel, i, h, send, row, col, source=None):
        here = chunk(left.at[panel, i], h)
        return remote(here if source is None else source, here, send, piece_sem.at[panel, i, h], row, col)

    def first_copy(i, h):
        return pass_on(0, i, h, root_sem.at[0, 0, i, h], r, at(i, 0), chunk(stage.at[0, i], h))

    def second_copy(i, h):
        return remote(
            chunk(stage.at[1, i], h), chunk(onward, h), root_sem.at[1, 0, i, h], onward_sem.at[h], r, at(i, 1)
        )

    def aside_copy(role, i, h):
        return remote(
            chunk(stage.at[role, i], h), chunk(aside, h), root_sem.at[role, 1, i, h], aside_sem.at[h], across, at(i, role)
        )

    def for_root_copies(do):
        def both(role, i, h, direct, own):
            if h in ASIDE:
                do(aside_copy(role, i, h))

            @pl.when(jnp.logical_not(jnp.logical_and(own, x == i)))
            def _():
                do(direct(i, h))

        for h in ORDER:
            @pl.when(first_root)
            def _():
                for i in range(PIECES):
                    both(0, i, h, first_copy, own_first)

            @pl.when(second_root)
            def _():
                for i in range(PIECES):
                    both(1, i, h, second_copy, own_second)

    def keep(condition, source, target, do):
        @pl.when(condition)
        def _():
            do(pltpu.make_async_copy(source, target, local_sem.at[2]))

    def keep_first(do):
        keep(own_first, stage.at[0, x], left.at[0, x], do)

    def keep_second(do):
        keep(own_second, stage.at[1, x], onward, do)

    def first_meta(peer):
        return remote(meta, metas.at[0], meta_send.at[0], meta_recv.at[0], *peer)

    def second_meta(peer):
        return remote(meta, metas.at[1], meta_send.at[1], meta_recv.at[1], *peer)

    def home_meta(peer):
        return remote(meta, root_meta, meta_send.at[4], meta_recv.at[4], *peer)

    shift_meta = remote(meta, metas.at[2], meta_send.at[2], meta_recv.at[2], below, c)
    if partial:
        upward_meta = remote(meta, below_meta, meta_send.at[3], meta_recv.at[3], above, c)

    def sent(n, send):
        many = z_flags.at[pl.ds(0, n)]
        remote(many, many, send, flag_recv.at[0], below, c).wait_send()

    slots = ROOM if partial else SLOTS
    parts = 2 if partial else 5

    def shift_copy(i):
        part = pl.ds(i * (slots // parts), slots // parts)
        source = packed if partial else blocks
        return remote(source.at[part], right.at[part], shift_send.at[i], shift_recv.at[i], below, c)

    def straight_first(h):
        return pass_on(0, x, h, cross_sem.at[h], r, other)

    def straight_second(h):
        return pass_on(1, x, h, cross_sem.at[h], below, other, chunk(onward, h))

    def to_near(h):
        return pass_on(1, x, h, near_sem.at[h], below, same, chunk(onward, h))

    def from_aside(role, h):
        return pass_on(role, x, h, cross_sem.at[h], across if role == 0 else across_below, other, chunk(aside, h))

    def x_copy(n, h):
        return pass_on(k, x, h, x_sem.at[n, h], r, at(ring[n], k))

    def core_copy(n, i, h):
        return pass_on(k, i, h, core_sem.at[n, h], r, at(x, 1 - k))

    def arrived(panel, i, h):
        pass_on(panel, i, h, core_sem.at[0, 0], r, at(x, 1 - k)).wait_recv()

    def landed(ref, h, sem):
        remote(chunk(ref, h), chunk(ref, h), core_sem.at[0, 0], sem.at[h], r, at(x, 1 - k)).wait_recv()

    def amount(condition, n):
        return jnp.where(condition, n, 0)

    sends = (
        5
        + amount(first_root, 8 + 15) - amount(own_first, 1)
        + amount(second_root, 8 + 16) - amount(own_second, 1)
        + amount(near_first, 1) + amount(aside_first, 1) + amount(near_second, 2) + amount(aside_second, 1)
    )
    if partial:
        sends = sends + 1 + 25 + amount(second_root, 15)
    pl.semaphore_wait(barrier, sends)

    if partial:
        upward_meta.start()

        @pl.when(second_root)
        def _():
            for peer in row_peers:
                home_meta(peer).start()
            root_meta[...] = meta[...]

    for_root_copies(lambda copy: copy.start())
    keep_first(lambda copy: copy.start())
    keep_second(lambda copy: copy.start())
    shift_meta.start()

    if not partial:
        for i in range(parts):
            shift_copy(i).start()

    @pl.when(first_root)
    def _():
        for peer in row_peers:
            first_meta(peer).start()
        metas[0] = meta[...]

    @pl.when(second_root)
    def _():
        for col in range(N_COL):
            second_meta((below, col)).start()

    keep_first(lambda copy: copy.wait())
    keep_second(lambda copy: copy.wait())

    def spread(h):
        for n in range(3):
            x_copy(n, h).start()
        core_copy(0, x, h).start()

    @pl.when(near_first)
    def _():
        for h in ORDER:
            @pl.when(jnp.logical_not(own_first))
            def _():
                arrived(0, x, h)

            if h in STRAIGHT:
                straight_first(h).start()
            spread(h)

    @pl.when(aside_first)
    def _():
        for h in ASIDE:
            landed(aside, h, aside_sem)
            from_aside(0, h).start()

    @pl.when(near_second)
    def _():
        for h in ORDER:
            @pl.when(jnp.logical_not(own_second))
            def _():
                landed(onward, h, onward_sem)

            if h in STRAIGHT:
                straight_second(h).start()
            to_near(h).start()

    @pl.when(aside_second)
    def _():
        for h in ASIDE:
            landed(aside, h, aside_sem)
            from_aside(1, h).start()

    def send_flags(peers, buffer, me, n):
        buffer[me] = flag_v[n]
        for peer in peers:
            remote(flag_v.at[n], buffer.at[me], flag_send.at[n], flag_recv.at[n], *peer).start()

    def join_flags(buffer, count, n):
        others = buffer.at[pl.ds(0, count - 1)]
        remote(others, others, flag_send.at[n], flag_recv.at[n], below, c).wait_recv()
        joined = buffer[0]
        for i in range(1, count):
            joined = jnp.maximum(joined, buffer[i])
        return joined

    wide_lane = lax.broadcasted_iota(jnp.int32, (SLOTS, 128), 1)
    wide_sub = lax.broadcasted_iota(jnp.int32, (SLOTS, 128), 0)

    line, column = own[0:1, :], own[1:2, :]

    def down(values):
        return jnp.sum(jnp.where(wide_lane == wide_sub, values, 0), axis=1, keepdims=True)

    def bits(rows, valid):
        return jnp.where(valid, jnp.left_shift(1, jnp.maximum(rows, 0)), 0)

    def union(keys, masks, wanted):
        return jnp.sum(jnp.where(down(keys) == wanted, down(masks), 0), axis=0, keepdims=True)

    def rank(chosen):
        return jnp.sum(jnp.where(wide_sub < wide_lane, down(jnp.where(chosen, 1, 0)), 0), axis=0, keepdims=True)

    def left_half(coords, which):
        lines, columns = coords[0:1, :], coords[1:2, :] - BROW * which
        inside = jnp.logical_and(lines >= 0, jnp.logical_and(columns >= 0, columns < BROW))
        return lines, jnp.where(inside, columns, -1), inside

    def needs_of(lines, columns, half_coords, output_lines, output_columns):
        left_lines, left_columns, inside = half_coords
        by_line = union(left_lines, bits(left_columns, inside), lines)
        by_column = union(output_columns, bits(output_lines, output_lines >= 0), columns)
        return jnp.logical_and(lines >= 0, jnp.bitwise_and(by_line, by_column) != 0)

    if partial:
        upward_meta.wait_recv()

        @pl.when(jnp.logical_not(second_root))
        def _():
            home_meta(row_peers[0]).wait_recv()

        theirs = below_meta[...]
        needed = needs_of(line, column, left_half(root_meta[...], below % 2), theirs[0:1, :], theirs[1:2, :])
        spot_sub = lax.broadcasted_iota(jnp.int32, (ROOM, 128), 0)
        spot_lane = lax.broadcasted_iota(jnp.int32, (ROOM, 128), 1)
        chosen = jnp.logical_and(needed, rank(needed) == spot_sub)
        slot = jnp.sum(jnp.where(chosen, spot_lane, 0), axis=1, keepdims=True)
        need_v[...] = jnp.broadcast_to(slot, (ROOM, 128))
        needs = pltpu.make_async_copy(need_v, need_s, local_sem.at[3])
        needs.start()
        total = jnp.sum(jnp.where(needed, 1, 0), axis=1, keepdims=True)
        flag_v[0] = jnp.broadcast_to(jnp.where(total > ROOM, 1, 0), (8, 128))
        needs.wait()
        for s in range(ROOM):
            packed[s] = held[jnp.clip(need_s[s, 0], 0, SLOTS - 1)]
        for i in range(parts):
            shift_copy(i).start()
        send_flags(chip_peers, chip_flags, x * 2 + k, 0)

    if partial:
        flag_v[1] = join_flags(chip_flags, 8, 0)
        send_flags(z_peers, z_flags, z, 1)

    @pl.when(jnp.logical_not(near_first))
    def _():
        for h in ORDER:
            arrived(k, x, h)
            spread(h)

    if partial:
        flag_v[2] = join_flags(z_flags, 16, 1)
        send_flags(y_peers, y_flags, y, 2)

    for h in ORDER:
        for n in range(3):
            arrived(k, ring[n], h)
            core_copy(1 + n, ring[n], h).start()

    @pl.when(jnp.logical_not(first_root))
    def _():
        first_meta(row_peers[0]).wait_recv()

    second_meta((below, c)).wait_recv()
    shift_meta.wait_recv()
    halves = [left_half(metas[p], r % 2) for p in range(2)]
    shift_line, shift_column = metas[2, 0:1, :], metas[2, 1:2, :]
    if partial:
        present = needs_of(shift_line, shift_column, halves[1], line, column)
        position = jnp.minimum(rank(present), ROOM - 1)
    else:
        present = shift_line >= 0
        position = lane[0:1, :]
    entries = []
    for p, (lines, columns) in enumerate(((line, column), (shift_line, shift_column))):
        left_lines, left_columns, inside = halves[p]
        meet = jnp.bitwise_and(
            union(left_columns, bits(left_lines, inside), line), union(columns, bits(lines, lines >= 0), column)
        )
        entries.append(jnp.where(line >= 0, meet, 0))
        entries.append(jnp.where(inside, p * 256 + left_columns * 16 + left_lines, 255))
        entries.append(jnp.minimum(rank(inside), HALF - 1))
    entries.append(jnp.where(line >= 0, column * 16 + line, 511))
    entries.append(jnp.where(present, 512 + shift_column * 16 + shift_line, 1023))
    entries.append(position)
    entries.append(jnp.maximum(line, 0) * 16)
    entries.append(jnp.maximum(column, 0) * 16)
    sub16 = lax.broadcasted_iota(jnp.int32, (16, 128), 0)
    table = jnp.zeros((16, 128), jnp.int32)
    for i, entry in enumerate(entries):
        table = jnp.where(sub16 == i, entry, table)
    plan[...] = table

    for h in ORDER:
        for i in range(PIECES):
            arrived(1 - k, i, h)

    if partial:
        flag[0, 0] = jnp.max(join_flags(y_flags, 4, 2))
        sent(7, flag_send.at[0])
        sent(15, flag_send.at[1])
        sent(3, flag_send.at[2])
    else:
        flag[0, 0] = 0

    for_root_copies(lambda copy: copy.wait_send())

    @pl.when(first_root)
    def _():
        sent(15, meta_send.at[0])

    @pl.when(second_root)
    def _():
        sent(16, meta_send.at[1])

    shift_meta.wait_send()
    if partial:
        upward_meta.wait_send()

        @pl.when(second_root)
        def _():
            sent(15, meta_send.at[4])

    @pl.when(near_first)
    def _():
        for h in STRAIGHT:
            straight_first(h).wait_send()

    @pl.when(near_second)
    def _():
        for h in STRAIGHT:
            straight_second(h).wait_send()
        for h in ORDER:
            to_near(h).wait_send()

    @pl.when(aside_first)
    def _():
        for h in ASIDE:
            from_aside(0, h).wait_send()

    @pl.when(aside_second)
    def _():
        for h in ASIDE:
            from_aside(1, h).wait_send()

    for h in ORDER:
        for n in range(3):
            x_copy(n, h).wait_send()
        core_copy(0, x, h).wait_send()
        for n in range(3):
            core_copy(1 + n, ring[n], h).wait_send()
    for i in range(parts):
        shift_copy(i).wait()


def gather(rows, cols, blocks, partial):
    any_space = pl.BlockSpec(memory_space=pl.ANY)
    scalars = pl.BlockSpec(memory_space=pltpu.SMEM)
    dma = pltpu.SemaphoreType.DMA
    tile = (8, 128)
    hops = len(CHUNKS)
    return pl.pallas_call(
        functools.partial(gather_kernel, partial),
        name="gather_needed" if partial else "gather_all",
        out_shape=(
            jax.ShapeDtypeStruct((2, PIECES, PIECE_ROWS, BS), jnp.bfloat16),
            jax.ShapeDtypeStruct((ROOM if partial else SLOTS, BS, BS), jnp.bfloat16),
            jax.ShapeDtypeStruct((16, 128), jnp.int32),
            jax.ShapeDtypeStruct((1, 1), jnp.int32),
        ),
        in_specs=[scalars, scalars, any_space],
        out_specs=(any_space, any_space, pl.BlockSpec(memory_space=pltpu.VMEM), scalars),
        scratch_shapes=[
            pltpu.VMEM((3, *tile), jnp.int32),
            pltpu.VMEM((SLOTS, BS, BS), jnp.bfloat16),
            pltpu.VMEM((2, PIECES, PIECE_ROWS, BS), jnp.bfloat16),
            pltpu.VMEM((ROOM, BS, BS), jnp.bfloat16),
            pltpu.VMEM(tile, jnp.int32),
            pltpu.VMEM(tile, jnp.int32),
            pltpu.VMEM(tile, jnp.int32),
            pltpu.VMEM(tile, jnp.int32),
            pltpu.SMEM(tile, jnp.int32),
            pltpu.VMEM((ROOM, 128), jnp.int32),
            pltpu.SMEM((ROOM, 128), jnp.int32),
            pltpu.VMEM((PIECE_ROWS, BS), jnp.bfloat16),
            pltpu.VMEM((PIECE_ROWS, BS), jnp.bfloat16),
            pltpu.VMEM((8, *tile), jnp.int32),
            pltpu.VMEM((16, *tile), jnp.int32),
            pltpu.VMEM((4, *tile), jnp.int32),
            pltpu.VMEM((3, *tile), jnp.int32),
            dma((4,)),
            dma((2, 2, PIECES, hops)),
            dma((2, PIECES, hops)),
            dma((hops,)),
            dma((hops,)),
            dma((hops,)),
            dma((hops,)),
            dma((3, hops)),
            dma((PIECES, hops)),
            dma((5,)),
            dma((5,)),
            dma((5,)),
            dma((5,)),
            dma((3,)),
            dma((3,)),
        ],
        compiler_params=pltpu.CompilerParams(
            collective_id=0 if partial else 1, has_side_effects=True, vmem_limit_bytes=GATHER_MIB * 1024 * 1024
        ),
    )(rows, cols, blocks)


GATHER_MIB = 62
MULTIPLY_MIB = 62


MEET, LEFT_CELL, LEFT_PLACE = (0, 3), (1, 4), (2, 5)
OWN_CELL, SHIFT_CELL, SHIFT_PLACE, LEFT_BASE, RIGHT_BASE = 6, 7, 8, 9, 10
LOWEST = 0x09AF


def multiply_kernel(
    plan, blocks, right, left, out,
    left_slot, right_slot, bit_s, where_s, slot_s, count_s,
    zeros, left_v, right_v, total, done, zero_sem, load_sem, store_sem,
):
    zeros[...] = jnp.zeros_like(zeros)
    clear = pltpu.make_async_copy(zeros, out, zero_sem)
    clear.start()
    for i in range(16):
        bit_s[(LOWEST << i & 0xFFFF) >> 12] = i
    count_s[0] = 0
    count_s[1] = 0

    @pl.loop(0, SLOTS, unroll=8)
    def _(t):
        for p in range(2):
            left_slot[plan[LEFT_CELL[p], t]] = plan[LEFT_PLACE[p], t]
        right_slot[plan[OWN_CELL, t]] = t
        right_slot[plan[SHIFT_CELL, t]] = plan[SHIFT_PLACE, t]

    def load(p, m, t):
        n = jnp.minimum(count_s[0], MEETINGS - 1)
        j = jnp.clip(left_slot[p * 256 + plan[LEFT_BASE, t] + m], 0, HALF - 1)
        piece = j // PER
        start = pl.multiple_of((j - piece * PER) * BS, BS)
        source = (blocks, right)[p]
        slot = jnp.clip(right_slot[p * 512 + plan[RIGHT_BASE, t] + m], 0, source.shape[0] - 1)
        pltpu.make_async_copy(left.at[p, piece, pl.ds(start, BS)], left_v.at[n], load_sem.at[0]).start()
        pltpu.make_async_copy(source.at[slot], right_v.at[n], load_sem.at[1]).start()
        where_s[n] = t
        count_s[0] = n + 1

    @pl.loop(0, SLOTS)
    def _(t):
        meet = [plan[MEET[p], t] for p in range(2)]

        @pl.when((meet[0] | meet[1]) != 0)
        def _():
            slot_s[count_s[1]] = t
            count_s[1] = count_s[1] + 1
            total[t] = jnp.zeros_like(total[t])
            for p in range(2):
                def each(bits):
                    lowest = bits & -bits
                    load(p, bit_s[((lowest * LOWEST) & 0xFFFF) >> 12], t)
                    return bits ^ lowest

                lax.while_loop(lambda bits: bits != 0, each, meet[p])

    n, slots = count_s[0], count_s[1]
    for u in range(GROUP):
        where_s[n + u] = SLOTS

    @pl.loop(0, n)
    def _(i):
        pltpu.make_async_copy(blocks.at[0], left_v.at[0], load_sem.at[0]).wait()
        pltpu.make_async_copy(blocks.at[0], right_v.at[0], load_sem.at[1]).wait()

    @pl.loop(0, (n + GROUP - 1) // GROUP)
    def _(g):
        products = [
            jnp.dot(left_v[g * GROUP + u], right_v[g * GROUP + u], preferred_element_type=jnp.float32)
            for u in range(GROUP)
        ]
        for u in range(GROUP):
            t = where_s[g * GROUP + u]
            total[t] = total[t] + products[u]

    clear.wait()

    @pl.loop(0, slots)
    def _(i):
        t = slot_s[i]
        done[i] = total[t].astype(jnp.bfloat16)
        pltpu.make_async_copy(done.at[i], out.at[t], store_sem).start()

    @pl.loop(0, slots)
    def _(i):
        pltpu.make_async_copy(done.at[0], out.at[0], store_sem).wait()


def multiply(plan, blocks, right, left):
    any_space = pl.BlockSpec(memory_space=pl.ANY)
    room = MEETINGS + GROUP
    return pl.pallas_call(
        multiply_kernel,
        name="multiply",
        out_shape=jax.ShapeDtypeStruct((SLOTS, BS, BS), jnp.bfloat16),
        in_specs=[pl.BlockSpec(memory_space=pltpu.SMEM), any_space, any_space, any_space],
        out_specs=any_space,
        scratch_shapes=[
            pltpu.SMEM((512,), jnp.int32),
            pltpu.SMEM((1024,), jnp.int32),
            pltpu.SMEM((16,), jnp.int32),
            pltpu.SMEM((room,), jnp.int32),
            pltpu.SMEM((SLOTS,), jnp.int32),
            pltpu.SMEM((2,), jnp.int32),
            pltpu.VMEM((SLOTS, BS, BS), jnp.bfloat16),
            pltpu.VMEM((room, BS, BS), jnp.bfloat16),
            pltpu.VMEM((room, BS, BS), jnp.bfloat16),
            pltpu.VMEM((SLOTS + 1, BS, BS), jnp.float32),
            pltpu.VMEM((SLOTS, BS, BS), jnp.bfloat16),
            pltpu.SemaphoreType.DMA,
            pltpu.SemaphoreType.DMA((2,)),
            pltpu.SemaphoreType.DMA,
        ],
        compiler_params=pltpu.CompilerParams(vmem_limit_bytes=MULTIPLY_MIB * 1024 * 1024),
    )(plan, blocks, right, left)


def product(rows, cols, blocks, partial):
    left, right, plan, flag = gather(rows, cols, blocks, partial)
    return multiply(plan, blocks, right, left), flag


def shards(blocks, block_rows, block_cols):
    blocks, rows, cols = blocks[0, 0], block_rows[0, 0], block_cols[0, 0]
    result, flag = product(rows, cols, blocks, True)
    result = lax.cond(flag[0, 0] > 0, lambda: product(rows, cols, blocks, False)[0], lambda: result)
    return result[None, None]


def solution(mesh):
    return jax.shard_map(
        shards,
        mesh=mesh,
        in_specs=(P("row", "col", None, None, None), P("row", "col", None), P("row", "col", None)),
        out_specs=P("row", "col", None, None, None),
        check_vma=False,
    )
```

```python
import functools

import jax
import jax.numpy as jnp
from jax import lax
from jax.experimental import pallas as pl
from jax.experimental.pallas import tpu as pltpu
from jax.sharding import PartitionSpec as P

MESH = pl.DeviceIdType.MESH
BS = 128
BROW = 13
HALF = 20
SLOTS = 40
ROOM = 16
N_ROW = 32
N_COL = 16
PIECES = 4
PER = HALF // PIECES
PIECE_ROWS = PER * BS
CHUNKS = ((0, 320), (320, PIECE_ROWS))
ASIDE = (0,)
STRAIGHT = (1,)
ORDER = (1, 0)
MEETINGS = 2 * 178
GROUP = 4


def gather_kernel(
    partial,
    rows_s, cols_s, blocks,
    left, right, plan, flag,
    metas, held, stage, packed, meta, below_meta, root_meta, order_v, order_s, need_v, need_s, onward, aside,
    chip_flags, z_flags, y_flags, flag_v,
    local_sem, root_sem, piece_sem, onward_sem, aside_sem, cross_sem, near_sem, x_sem, core_sem,
    shift_send, shift_recv, meta_send, meta_recv, flag_send, flag_recv,
):
    r, c = lax.axis_index("row"), lax.axis_index("col")
    y, zl = r // 8, r % 8
    zh, x, k = c // 8, (c // 2) % 4, c % 2
    z = zh * 8 + zl
    above, below = (r + 1) % N_ROW, (r + N_ROW - 1) % N_ROW

    def mirrored(row):
        return row + 8 * (3 - 2 * (row // 8))

    def home(row):
        return row // 16

    across = mirrored(r)
    across_below = (across + N_ROW - 1) % N_ROW
    first_root = c == r // 2
    second_root = c == below // 2
    first_panel, second_panel = k == 0, k == 1
    own_first = jnp.logical_and(first_root, first_panel)
    own_second = jnp.logical_and(second_root, second_panel)
    near = zh == home(r)
    far = jnp.logical_not(near)
    near_first = jnp.logical_and(first_panel, near)
    aside_first = jnp.logical_and(first_panel, far)
    near_second = jnp.logical_and(second_panel, zh == home(below))
    aside_second = jnp.logical_and(second_panel, zh == home(across_below))

    def at(x_of, k_of, zh_of=zh):
        return zh_of * 8 + x_of * 2 + k_of

    same, other = at(x, k), at(x, k, 1 - zh)
    ring = [(x + d) % 4 for d in (1, 3, 2)]
    chip_peers = [(r, zh * 8 + (x * 2 + k + d) % 8) for d in range(1, 8)]
    z_peers = [(y * 8 + (z + d) % 8, ((z + d) % 16) // 8 * 8 + x * 2 + k) for d in range(1, 16)]
    y_peers = [((y + d) % 4 * 8 + zl, c) for d in range(1, 4)]
    row_peers = [(r, (c + d) % N_COL) for d in range(1, N_COL)]
    barrier = pltpu.get_barrier_semaphore()

    def greet(row, col):
        pl.semaphore_signal(barrier, inc=1, device_id=(row, col), device_id_type=MESH)

    def greet_if(condition, row, col):
        @pl.when(condition)
        def _():
            greet(row, col)

    greet_if(jnp.logical_and(first_panel, far), r, other)
    greet_if(jnp.logical_and(first_panel, far), across, other)
    greet_if(jnp.logical_and(second_panel, far), above, other)
    greet_if(jnp.logical_and(second_panel, far), mirrored(above), other)
    greet(above, r // 2)
    greet_if(jnp.logical_not(first_root), r, r // 2)
    greet_if(jnp.logical_and(second_panel, near), above, same)
    greet(above, c)
    greet_if(jnp.logical_and(near_first, jnp.logical_not(own_first)), r, r // 2)
    greet_if(aside_first, across, across // 2)
    greet_if(jnp.logical_and(near_second, jnp.logical_not(own_second)), r, below // 2)
    greet_if(aside_second, across, across_below // 2)
    if partial:
        greet_if(jnp.logical_not(second_root), r, below // 2)
        greet(below, c)
        for peer in z_peers + y_peers + chip_peers:
            greet(*peer)
    greet(r, at(x, 1 - k))
    for x_of in ring:
        greet(r, at(x_of, k))

    is_root = jnp.logical_or(first_root, second_root)

    def fetch():
        return pltpu.make_async_copy(blocks, held, local_sem.at[0])

    if partial:
        fetch().start()
    else:
        pl.when(is_root)(lambda: fetch().start())

    lane = lax.broadcasted_iota(jnp.int32, (8, 128), 1)
    sub = lax.broadcasted_iota(jnp.int32, (8, 128), 0)

    def place(t, carry):
        n0, n1, own, order = carry
        a, b = rows_s[t], cols_s[t]
        half = jnp.where(b >= BROW, 1, 0)
        live = jnp.where(a >= 0, 1, 0)
        spot = jnp.where(a >= 0, jnp.where(b >= BROW, n1, n0), 127)
        own = jnp.where(lane == t, jnp.where(sub == 0, a, b), own)
        order = jnp.where(jnp.logical_and(lane == spot, sub == half), t, order)
        return n0 + live * (1 - half), n1 + live * half, own, order

    zero = jnp.zeros((8, 128), jnp.int32)
    _, _, own, order = lax.fori_loop(0, SLOTS, place, (jnp.int32(0), jnp.int32(0), zero - 1, zero))
    meta[...] = own

    @pl.when(is_root)
    def _():
        order_v[...] = order
        to_scalars = pltpu.make_async_copy(order_v, order_s, local_sem.at[1])
        to_scalars.start()
        to_scalars.wait()

    if partial:
        fetch().wait()
    else:
        pl.when(is_root)(lambda: fetch().wait())

    def pack(role, half):
        for i in range(PIECES):
            for j in range(PER):
                stage[role, i, j * BS:(j + 1) * BS, :] = held[jnp.clip(order_s[half, i * PER + j], 0, SLOTS - 1)].T

    @pl.when(first_root)
    def _():
        pack(0, r % 2)

    @pl.when(second_root)
    def _():
        pack(1, below % 2)

    def remote(src, dst, send, recv, row, col):
        return pltpu.make_async_remote_copy(
            src_ref=src, dst_ref=dst, send_sem=send, recv_sem=recv, device_id=(row, col), device_id_type=MESH
        )

    def chunk(ref, h):
        first, last = CHUNKS[h]
        return ref.at[pl.ds(first, last - first)]

    def pass_on(panel, i, h, send, row, col, source=None):
        here = chunk(left.at[panel, i], h)
        return remote(here if source is None else source, here, send, piece_sem.at[panel, i, h], row, col)

    def first_copy(i, h):
        return pass_on(0, i, h, root_sem.at[0, 0, i, h], r, at(i, 0), chunk(stage.at[0, i], h))

    def second_copy(i, h):
        return remote(
            chunk(stage.at[1, i], h), chunk(onward, h), root_sem.at[1, 0, i, h], onward_sem.at[h], r, at(i, 1)
        )

    def aside_copy(role, i, h):
        return remote(
            chunk(stage.at[role, i], h), chunk(aside, h), root_sem.at[role, 1, i, h], aside_sem.at[h], across, at(i, role)
        )

    def for_root_copies(do):
        def both(role, i, h, direct, own):
            if h in ASIDE:
                do(aside_copy(role, i, h))

            @pl.when(jnp.logical_not(jnp.logical_and(own, x == i)))
            def _():
                do(direct(i, h))

        for h in ORDER:
            @pl.when(second_root)
            def _():
                for i in range(PIECES):
                    both(1, i, h, second_copy, own_second)

            @pl.when(first_root)
            def _():
                for i in range(PIECES):
                    both(0, i, h, first_copy, own_first)

    def keep(condition, source, target, do):
        @pl.when(condition)
        def _():
            do(pltpu.make_async_copy(source, target, local_sem.at[2]))

    def keep_first(do):
        keep(own_first, stage.at[0, x], left.at[0, x], do)

    def keep_second(do):
        keep(own_second, stage.at[1, x], onward, do)

    def first_meta(peer):
        return remote(meta, metas.at[0], meta_send.at[0], meta_recv.at[0], *peer)

    def second_meta(peer):
        return remote(meta, metas.at[1], meta_send.at[1], meta_recv.at[1], *peer)

    def home_meta(peer):
        return remote(meta, root_meta, meta_send.at[4], meta_recv.at[4], *peer)

    shift_meta = remote(meta, metas.at[2], meta_send.at[2], meta_recv.at[2], below, c)
    if partial:
        upward_meta = remote(meta, below_meta, meta_send.at[3], meta_recv.at[3], above, c)

    def sent(n, send):
        many = z_flags.at[pl.ds(0, n)]
        remote(many, many, send, flag_recv.at[0], below, c).wait_send()

    slots = ROOM if partial else SLOTS
    parts = 2 if partial else 5

    def shift_copy(i):
        part = pl.ds(i * (slots // parts), slots // parts)
        source = packed if partial else blocks
        return remote(source.at[part], right.at[part], shift_send.at[i], shift_recv.at[i], below, c)

    def straight_first(h):
        return pass_on(0, x, h, cross_sem.at[h], r, other)

    def straight_second(h):
        return pass_on(1, x, h, cross_sem.at[h], below, other, chunk(onward, h))

    def to_near(h):
        return pass_on(1, x, h, near_sem.at[h], below, same, chunk(onward, h))

    def from_aside(role, h):
        return pass_on(role, x, h, cross_sem.at[h], across if role == 0 else across_below, other, chunk(aside, h))

    def x_copy(n, h):
        return pass_on(k, x, h, x_sem.at[n, h], r, at(ring[n], k))

    def core_copy(n, i, h):
        return pass_on(k, i, h, core_sem.at[n, h], r, at(x, 1 - k))

    def arrived(panel, i, h):
        pass_on(panel, i, h, core_sem.at[0, 0], r, at(x, 1 - k)).wait_recv()

    def landed(ref, h, sem):
        remote(chunk(ref, h), chunk(ref, h), core_sem.at[0, 0], sem.at[h], r, at(x, 1 - k)).wait_recv()

    def amount(condition, n):
        return jnp.where(condition, n, 0)

    sends = (
        5
        + amount(first_root, 8 + 15) - amount(own_first, 1)
        + amount(second_root, 8 + 16) - amount(own_second, 1)
        + amount(near_first, 1) + amount(aside_first, 1) + amount(near_second, 2) + amount(aside_second, 1)
    )
    if partial:
        sends = sends + 1 + 25 + amount(second_root, 15)
    pl.semaphore_wait(barrier, sends)

    if partial:
        upward_meta.start()

        @pl.when(second_root)
        def _():
            for peer in row_peers:
                home_meta(peer).start()
            root_meta[...] = meta[...]

    for_root_copies(lambda copy: copy.start())
    keep_first(lambda copy: copy.start())
    keep_second(lambda copy: copy.start())
    shift_meta.start()

    if not partial:
        for i in range(parts):
            shift_copy(i).start()

    @pl.when(first_root)
    def _():
        for peer in row_peers:
            first_meta(peer).start()
        metas[0] = meta[...]

    @pl.when(second_root)
    def _():
        for col in range(N_COL):
            second_meta((below, col)).start()

    keep_first(lambda copy: copy.wait())
    keep_second(lambda copy: copy.wait())

    def spread(h):
        for n in range(3):
            x_copy(n, h).start()
        core_copy(0, x, h).start()

    @pl.when(near_first)
    def _():
        for h in ORDER:
            @pl.when(jnp.logical_not(own_first))
            def _():
                arrived(0, x, h)

            if h in STRAIGHT:
                straight_first(h).start()
            spread(h)

    @pl.when(aside_first)
    def _():
        for h in ASIDE:
            landed(aside, h, aside_sem)
            from_aside(0, h).start()

    @pl.when(near_second)
    def _():
        for h in ORDER:
            @pl.when(jnp.logical_not(own_second))
            def _():
                landed(onward, h, onward_sem)

            if h in STRAIGHT:
                straight_second(h).start()
            to_near(h).start()

    @pl.when(aside_second)
    def _():
        for h in ASIDE:
            landed(aside, h, aside_sem)
            from_aside(1, h).start()

    def send_flags(peers, buffer, me, n):
        buffer[me] = flag_v[n]
        for peer in peers:
            remote(flag_v.at[n], buffer.at[me], flag_send.at[n], flag_recv.at[n], *peer).start()

    def join_flags(buffer, count, n):
        others = buffer.at[pl.ds(0, count - 1)]
        remote(others, others, flag_send.at[n], flag_recv.at[n], below, c).wait_recv()
        joined = buffer[0]
        for i in range(1, count):
            joined = jnp.maximum(joined, buffer[i])
        return joined

    wide_lane = lax.broadcasted_iota(jnp.int32, (SLOTS, 128), 1)
    wide_sub = lax.broadcasted_iota(jnp.int32, (SLOTS, 128), 0)

    line, column = own[0:1, :], own[1:2, :]

    def down(values):
        return jnp.sum(jnp.where(wide_lane == wide_sub, values, 0), axis=1, keepdims=True)

    def bits(rows, valid):
        return jnp.where(valid, jnp.left_shift(1, jnp.maximum(rows, 0)), 0)

    def union(keys, masks, wanted):
        return jnp.sum(jnp.where(down(keys) == wanted, down(masks), 0), axis=0, keepdims=True)

    def rank(chosen):
        return jnp.sum(jnp.where(wide_sub < wide_lane, down(jnp.where(chosen, 1, 0)), 0), axis=0, keepdims=True)

    def left_half(coords, which):
        lines, columns = coords[0:1, :], coords[1:2, :] - BROW * which
        inside = jnp.logical_and(lines >= 0, jnp.logical_and(columns >= 0, columns < BROW))
        return lines, jnp.where(inside, columns, -1), inside

    def needs_of(lines, columns, half_coords, output_lines, output_columns):
        left_lines, left_columns, inside = half_coords
        by_line = union(left_lines, bits(left_columns, inside), lines)
        by_column = union(output_columns, bits(output_lines, output_lines >= 0), columns)
        return jnp.logical_and(lines >= 0, jnp.bitwise_and(by_line, by_column) != 0)

    if partial:
        upward_meta.wait_recv()

        @pl.when(jnp.logical_not(second_root))
        def _():
            home_meta(row_peers[0]).wait_recv()

        theirs = below_meta[...]
        needed = needs_of(line, column, left_half(root_meta[...], below % 2), theirs[0:1, :], theirs[1:2, :])
        spot_sub = lax.broadcasted_iota(jnp.int32, (ROOM, 128), 0)
        spot_lane = lax.broadcasted_iota(jnp.int32, (ROOM, 128), 1)
        chosen = jnp.logical_and(needed, rank(needed) == spot_sub)
        slot = jnp.sum(jnp.where(chosen, spot_lane, 0), axis=1, keepdims=True)
        need_v[...] = jnp.broadcast_to(slot, (ROOM, 128))
        needs = pltpu.make_async_copy(need_v, need_s, local_sem.at[3])
        needs.start()
        total = jnp.sum(jnp.where(needed, 1, 0), axis=1, keepdims=True)
        flag_v[0] = jnp.broadcast_to(jnp.where(total > ROOM, 1, 0), (8, 128))
        needs.wait()
        for s in range(ROOM):
            packed[s] = held[jnp.clip(need_s[s, 0], 0, SLOTS - 1)]
        for i in range(parts):
            shift_copy(i).start()
        send_flags(chip_peers, chip_flags, x * 2 + k, 0)

    if partial:
        flag_v[1] = join_flags(chip_flags, 8, 0)
        send_flags(z_peers, z_flags, z, 1)

    @pl.when(jnp.logical_not(near_first))
    def _():
        for h in ORDER:
            arrived(k, x, h)
            spread(h)

    if partial:
        flag_v[2] = join_flags(z_flags, 16, 1)
        send_flags(y_peers, y_flags, y, 2)

    for h in ORDER:
        for n in range(3):
            arrived(k, ring[n], h)
            core_copy(1 + n, ring[n], h).start()

    @pl.when(jnp.logical_not(first_root))
    def _():
        first_meta(row_peers[0]).wait_recv()

    second_meta((below, c)).wait_recv()
    shift_meta.wait_recv()
    halves = [left_half(metas[p], r % 2) for p in range(2)]
    shift_line, shift_column = metas[2, 0:1, :], metas[2, 1:2, :]
    if partial:
        present = needs_of(shift_line, shift_column, halves[1], line, column)
        position = jnp.minimum(rank(present), ROOM - 1)
    else:
        present = shift_line >= 0
        position = lane[0:1, :]
    entries = []
    for p, (lines, columns) in enumerate(((line, column), (shift_line, shift_column))):
        left_lines, left_columns, inside = halves[p]
        meet = jnp.bitwise_and(
            union(left_columns, bits(left_lines, inside), line), union(columns, bits(lines, lines >= 0), column)
        )
        entries.append(jnp.where(line >= 0, meet, 0))
        entries.append(jnp.where(inside, p * 256 + left_columns * 16 + left_lines, 255))
        entries.append(jnp.minimum(rank(inside), HALF - 1))
    entries.append(jnp.where(line >= 0, column * 16 + line, 511))
    entries.append(jnp.where(present, 512 + shift_column * 16 + shift_line, 1023))
    entries.append(position)
    entries.append(jnp.maximum(line, 0) * 16)
    entries.append(jnp.maximum(column, 0) * 16)
    sub16 = lax.broadcasted_iota(jnp.int32, (16, 128), 0)
    table = jnp.zeros((16, 128), jnp.int32)
    for i, entry in enumerate(entries):
        table = jnp.where(sub16 == i, entry, table)
    plan[...] = table

    for h in ORDER:
        for i in range(PIECES):
            arrived(1 - k, i, h)

    if partial:
        flag[0, 0] = jnp.max(join_flags(y_flags, 4, 2))
        sent(7, flag_send.at[0])
        sent(15, flag_send.at[1])
        sent(3, flag_send.at[2])
    else:
        flag[0, 0] = 0

    for_root_copies(lambda copy: copy.wait_send())

    @pl.when(first_root)
    def _():
        sent(15, meta_send.at[0])

    @pl.when(second_root)
    def _():
        sent(16, meta_send.at[1])

    shift_meta.wait_send()
    if partial:
        upward_meta.wait_send()

        @pl.when(second_root)
        def _():
            sent(15, meta_send.at[4])

    @pl.when(near_first)
    def _():
        for h in STRAIGHT:
            straight_first(h).wait_send()

    @pl.when(near_second)
    def _():
        for h in STRAIGHT:
            straight_second(h).wait_send()
        for h in ORDER:
            to_near(h).wait_send()

    @pl.when(aside_first)
    def _():
        for h in ASIDE:
            from_aside(0, h).wait_send()

    @pl.when(aside_second)
    def _():
        for h in ASIDE:
            from_aside(1, h).wait_send()

    for h in ORDER:
        for n in range(3):
            x_copy(n, h).wait_send()
        core_copy(0, x, h).wait_send()
        for n in range(3):
            core_copy(1 + n, ring[n], h).wait_send()
    for i in range(parts):
        shift_copy(i).wait()


def gather(rows, cols, blocks, partial):
    any_space = pl.BlockSpec(memory_space=pl.ANY)
    scalars = pl.BlockSpec(memory_space=pltpu.SMEM)
    dma = pltpu.SemaphoreType.DMA
    tile = (8, 128)
    hops = len(CHUNKS)
    return pl.pallas_call(
        functools.partial(gather_kernel, partial),
        name="gather_needed" if partial else "gather_all",
        out_shape=(
            jax.ShapeDtypeStruct((2, PIECES, PIECE_ROWS, BS), jnp.bfloat16),
            jax.ShapeDtypeStruct((ROOM if partial else SLOTS, BS, BS), jnp.bfloat16),
            jax.ShapeDtypeStruct((16, 128), jnp.int32),
            jax.ShapeDtypeStruct((1, 1), jnp.int32),
        ),
        in_specs=[scalars, scalars, any_space],
        out_specs=(any_space, any_space, pl.BlockSpec(memory_space=pltpu.VMEM), scalars),
        scratch_shapes=[
            pltpu.VMEM((3, *tile), jnp.int32),
            pltpu.VMEM((SLOTS, BS, BS), jnp.bfloat16),
            pltpu.VMEM((2, PIECES, PIECE_ROWS, BS), jnp.bfloat16),
            pltpu.VMEM((ROOM, BS, BS), jnp.bfloat16),
            pltpu.VMEM(tile, jnp.int32),
            pltpu.VMEM(tile, jnp.int32),
            pltpu.VMEM(tile, jnp.int32),
            pltpu.VMEM(tile, jnp.int32),
            pltpu.SMEM(tile, jnp.int32),
            pltpu.VMEM((ROOM, 128), jnp.int32),
            pltpu.SMEM((ROOM, 128), jnp.int32),
            pltpu.VMEM((PIECE_ROWS, BS), jnp.bfloat16),
            pltpu.VMEM((PIECE_ROWS, BS), jnp.bfloat16),
            pltpu.VMEM((8, *tile), jnp.int32),
            pltpu.VMEM((16, *tile), jnp.int32),
            pltpu.VMEM((4, *tile), jnp.int32),
            pltpu.VMEM((3, *tile), jnp.int32),
            dma((4,)),
            dma((2, 2, PIECES, hops)),
            dma((2, PIECES, hops)),
            dma((hops,)),
            dma((hops,)),
            dma((hops,)),
            dma((hops,)),
            dma((3, hops)),
            dma((PIECES, hops)),
            dma((5,)),
            dma((5,)),
            dma((5,)),
            dma((5,)),
            dma((3,)),
            dma((3,)),
        ],
        compiler_params=pltpu.CompilerParams(
            collective_id=0 if partial else 1, has_side_effects=True, vmem_limit_bytes=GATHER_MIB * 1024 * 1024
        ),
    )(rows, cols, blocks)


GATHER_MIB = 62
MULTIPLY_MIB = 62


MEET, LEFT_CELL, LEFT_PLACE = (0, 3), (1, 4), (2, 5)
OWN_CELL, SHIFT_CELL, SHIFT_PLACE, LEFT_BASE, RIGHT_BASE = 6, 7, 8, 9, 10
LOWEST = 0x09AF


def multiply_kernel(
    plan, blocks, right, left, out,
    left_slot, right_slot, bit_s, where_s, slot_s, count_s,
    zeros, left_v, right_v, total, done, zero_sem, load_sem, store_sem,
):
    zeros[...] = jnp.zeros_like(zeros)
    clear = pltpu.make_async_copy(zeros, out, zero_sem)
    clear.start()
    for i in range(16):
        bit_s[(LOWEST << i & 0xFFFF) >> 12] = i
    count_s[0] = 0
    count_s[1] = 0

    @pl.loop(0, SLOTS, unroll=8)
    def _(t):
        for p in range(2):
            left_slot[plan[LEFT_CELL[p], t]] = plan[LEFT_PLACE[p], t]
        right_slot[plan[OWN_CELL, t]] = t
        right_slot[plan[SHIFT_CELL, t]] = plan[SHIFT_PLACE, t]

    def load(p, m, t):
        n = jnp.minimum(count_s[0], MEETINGS - 1)
        j = jnp.clip(left_slot[p * 256 + plan[LEFT_BASE, t] + m], 0, HALF - 1)
        piece = j // PER
        start = pl.multiple_of((j - piece * PER) * BS, BS)
        source = (blocks, right)[p]
        slot = jnp.clip(right_slot[p * 512 + plan[RIGHT_BASE, t] + m], 0, source.shape[0] - 1)
        pltpu.make_async_copy(left.at[p, piece, pl.ds(start, BS)], left_v.at[n], load_sem.at[0]).start()
        pltpu.make_async_copy(source.at[slot], right_v.at[n], load_sem.at[1]).start()
        where_s[n] = t
        count_s[0] = n + 1

    @pl.loop(0, SLOTS)
    def _(t):
        meet = [plan[MEET[p], t] for p in range(2)]

        @pl.when((meet[0] | meet[1]) != 0)
        def _():
            slot_s[count_s[1]] = t
            count_s[1] = count_s[1] + 1
            total[t] = jnp.zeros_like(total[t])
            for p in range(2):
                def each(bits):
                    lowest = bits & -bits
                    load(p, bit_s[((lowest * LOWEST) & 0xFFFF) >> 12], t)
                    return bits ^ lowest

                lax.while_loop(lambda bits: bits != 0, each, meet[p])

    n, slots = count_s[0], count_s[1]
    for u in range(GROUP):
        where_s[n + u] = SLOTS

    @pl.loop(0, n)
    def _(i):
        pltpu.make_async_copy(blocks.at[0], left_v.at[0], load_sem.at[0]).wait()
        pltpu.make_async_copy(blocks.at[0], right_v.at[0], load_sem.at[1]).wait()

    @pl.loop(0, (n + GROUP - 1) // GROUP)
    def _(g):
        products = [
            jnp.dot(left_v[g * GROUP + u], right_v[g * GROUP + u], preferred_element_type=jnp.float32)
            for u in range(GROUP)
        ]
        for u in range(GROUP):
            t = where_s[g * GROUP + u]
            total[t] = total[t] + products[u]

    clear.wait()

    @pl.loop(0, slots)
    def _(i):
        t = slot_s[i]
        done[i] = total[t].astype(jnp.bfloat16)
        pltpu.make_async_copy(done.at[i], out.at[t], store_sem).start()

    @pl.loop(0, slots)
    def _(i):
        pltpu.make_async_copy(done.at[0], out.at[0], store_sem).wait()


def multiply(plan, blocks, right, left):
    any_space = pl.BlockSpec(memory_space=pl.ANY)
    room = MEETINGS + GROUP
    return pl.pallas_call(
        multiply_kernel,
        name="multiply",
        out_shape=jax.ShapeDtypeStruct((SLOTS, BS, BS), jnp.bfloat16),
        in_specs=[pl.BlockSpec(memory_space=pltpu.SMEM), any_space, any_space, any_space],
        out_specs=any_space,
        scratch_shapes=[
            pltpu.SMEM((512,), jnp.int32),
            pltpu.SMEM((1024,), jnp.int32),
            pltpu.SMEM((16,), jnp.int32),
            pltpu.SMEM((room,), jnp.int32),
            pltpu.SMEM((SLOTS,), jnp.int32),
            pltpu.SMEM((2,), jnp.int32),
            pltpu.VMEM((SLOTS, BS, BS), jnp.bfloat16),
            pltpu.VMEM((room, BS, BS), jnp.bfloat16),
            pltpu.VMEM((room, BS, BS), jnp.bfloat16),
            pltpu.VMEM((SLOTS + 1, BS, BS), jnp.float32),
            pltpu.VMEM((SLOTS, BS, BS), jnp.bfloat16),
            pltpu.SemaphoreType.DMA,
            pltpu.SemaphoreType.DMA((2,)),
            pltpu.SemaphoreType.DMA,
        ],
        compiler_params=pltpu.CompilerParams(vmem_limit_bytes=MULTIPLY_MIB * 1024 * 1024),
    )(plan, blocks, right, left)


def product(rows, cols, blocks, partial):
    left, right, plan, flag = gather(rows, cols, blocks, partial)
    return multiply(plan, blocks, right, left), flag


def shards(blocks, block_rows, block_cols):
    blocks, rows, cols = blocks[0, 0], block_rows[0, 0], block_cols[0, 0]
    result, flag = product(rows, cols, blocks, True)
    result = lax.cond(flag[0, 0] > 0, lambda: product(rows, cols, blocks, False)[0], lambda: result)
    return result[None, None]


def solution(mesh):
    return jax.shard_map(
        shards,
        mesh=mesh,
        in_specs=(P("row", "col", None, None, None), P("row", "col", None), P("row", "col", None)),
        out_specs=P("row", "col", None, None, None),
        check_vma=False,
    )
```

```python
import functools

import jax
import jax.numpy as jnp
from jax import lax
from jax.experimental import pallas as pl
from jax.experimental.pallas import tpu as pltpu
from jax.sharding import PartitionSpec as P

MESH = pl.DeviceIdType.MESH
BS = 128
BROW = 13
HALF = 20
SLOTS = 40
ROOM = 16
N_ROW = 32
N_COL = 16
PIECES = 4
PER = HALF // PIECES
PIECE_ROWS = PER * BS
CHUNKS = ((0, 320), (320, PIECE_ROWS))
ASIDE = (0,)
STRAIGHT = (1,)
ORDER = (1, 0)
MEETINGS = 2 * 178
GROUP = 4


def gather_kernel(
    partial,
    rows_s, cols_s, blocks,
    left, right, plan, flag,
    plan_v, metas, held, stage, packed, meta, below_meta, root_meta, order_v, order_s, need_v, need_s, onward, aside,
    chip_flags, z_flags, y_flags, flag_v,
    local_sem, root_sem, piece_sem, onward_sem, aside_sem, cross_sem, near_sem, x_sem, core_sem,
    shift_send, shift_recv, meta_send, meta_recv, flag_send, flag_recv,
):
    r, c = lax.axis_index("row"), lax.axis_index("col")
    y, zl = r // 8, r % 8
    zh, x, k = c // 8, (c // 2) % 4, c % 2
    z = zh * 8 + zl
    above, below = (r + 1) % N_ROW, (r + N_ROW - 1) % N_ROW

    def mirrored(row):
        return row + 8 * (3 - 2 * (row // 8))

    def home(row):
        return row // 16

    across = mirrored(r)
    across_below = (across + N_ROW - 1) % N_ROW
    aside_to, aside_of = mirrored(below), (across + 1) % N_ROW
    first_root = c == r // 2
    second_root = c == below // 2
    first_panel, second_panel = k == 0, k == 1
    own_first = jnp.logical_and(first_root, first_panel)
    own_second = jnp.logical_and(second_root, second_panel)
    near = zh == home(r)
    far = jnp.logical_not(near)
    near_first = jnp.logical_and(first_panel, near)
    aside_first = jnp.logical_and(first_panel, zh == home(aside_of))
    near_second = jnp.logical_and(second_panel, zh == home(below))
    aside_second = jnp.logical_and(second_panel, zh == home(across_below))

    def at(x_of, k_of, zh_of=zh):
        return zh_of * 8 + x_of * 2 + k_of

    same, other = at(x, k), at(x, k, 1 - zh)
    ring = [(x + d) % 4 for d in (1, 3, 2)]
    chip_peers = [(r, zh * 8 + (x * 2 + k + d) % 8) for d in range(1, 8)]
    z_peers = [(y * 8 + (z + d) % 8, ((z + d) % 16) // 8 * 8 + x * 2 + k) for d in range(1, 16)]
    y_peers = [((y + d) % 4 * 8 + zl, c) for d in range(1, 4)]
    row_peers = [(r, (c + d) % N_COL) for d in range(1, N_COL)]
    barrier = pltpu.get_barrier_semaphore()

    def greet(row, col):
        pl.semaphore_signal(barrier, inc=1, device_id=(row, col), device_id_type=MESH)

    def greet_if(condition, row, col):
        @pl.when(condition)
        def _():
            greet(row, col)

    greet_if(jnp.logical_and(first_panel, far), r, other)
    greet_if(jnp.logical_and(first_panel, far), aside_to, other)
    greet_if(jnp.logical_and(second_panel, far), above, other)
    greet_if(jnp.logical_and(second_panel, far), mirrored(above), other)
    greet(above, r // 2)
    greet_if(jnp.logical_not(first_root), r, r // 2)
    greet_if(jnp.logical_and(second_panel, near), above, same)
    greet(above, c)
    greet_if(jnp.logical_and(near_first, jnp.logical_not(own_first)), r, r // 2)
    greet_if(aside_first, aside_of, aside_of // 2)
    greet_if(jnp.logical_and(near_second, jnp.logical_not(own_second)), r, below // 2)
    greet_if(aside_second, across, across_below // 2)
    if partial:
        greet_if(jnp.logical_not(second_root), r, below // 2)
        greet(below, c)
        for peer in z_peers + y_peers + chip_peers:
            greet(*peer)
    greet(r, at(x, 1 - k))
    for x_of in ring:
        greet(r, at(x_of, k))

    is_root = jnp.logical_or(first_root, second_root)

    def fetch():
        return pltpu.make_async_copy(blocks, held, local_sem.at[0])

    if partial:
        fetch().start()
    else:
        pl.when(is_root)(lambda: fetch().start())

    lane = lax.broadcasted_iota(jnp.int32, (8, 128), 1)
    sub = lax.broadcasted_iota(jnp.int32, (8, 128), 0)

    def place(t, carry):
        n0, n1, own, order = carry
        a, b = rows_s[t], cols_s[t]
        half = jnp.where(b >= BROW, 1, 0)
        live = jnp.where(a >= 0, 1, 0)
        spot = jnp.where(a >= 0, jnp.where(b >= BROW, n1, n0), 127)
        own = jnp.where(lane == t, jnp.where(sub == 0, a, b), own)
        order = jnp.where(jnp.logical_and(lane == spot, sub == half), t, order)
        return n0 + live * (1 - half), n1 + live * half, own, order

    zero = jnp.zeros((8, 128), jnp.int32)
    _, _, own, order = lax.fori_loop(0, SLOTS, place, (jnp.int32(0), jnp.int32(0), zero - 1, zero))
    meta[...] = own

    @pl.when(is_root)
    def _():
        order_v[...] = order
        to_scalars = pltpu.make_async_copy(order_v, order_s, local_sem.at[1])
        to_scalars.start()
        to_scalars.wait()

    if partial:
        fetch().wait()
    else:
        pl.when(is_root)(lambda: fetch().wait())

    def pack(role, half):
        for i in range(PIECES):
            for j in range(PER):
                stage[role, i, j * BS:(j + 1) * BS, :] = held[jnp.clip(order_s[half, i * PER + j], 0, SLOTS - 1)].T

    @pl.when(first_root)
    def _():
        pack(0, r % 2)

    @pl.when(second_root)
    def _():
        pack(1, below % 2)

    def remote(src, dst, send, recv, row, col):
        return pltpu.make_async_remote_copy(
            src_ref=src, dst_ref=dst, send_sem=send, recv_sem=recv, device_id=(row, col), device_id_type=MESH
        )

    def chunk(ref, h):
        first, last = CHUNKS[h]
        return ref.at[pl.ds(first, last - first)]

    def pass_on(panel, i, h, send, row, col, source=None):
        here = chunk(left.at[panel, i], h)
        return remote(here if source is None else source, here, send, piece_sem.at[panel, i, h], row, col)

    def first_copy(i, h):
        return pass_on(0, i, h, root_sem.at[0, 0, i, h], r, at(i, 0), chunk(stage.at[0, i], h))

    def second_copy(i, h):
        return remote(
            chunk(stage.at[1, i], h), chunk(onward, h), root_sem.at[1, 0, i, h], onward_sem.at[h], r, at(i, 1)
        )

    def aside_copy(role, i, h):
        return remote(
            chunk(stage.at[role, i], h), chunk(aside, h), root_sem.at[role, 1, i, h], aside_sem.at[h],
            across if role else aside_to, at(i, role),
        )

    def for_root_copies(do):
        def both(role, i, h, direct, own):
            if h in ASIDE:
                do(aside_copy(role, i, h))

            @pl.when(jnp.logical_not(jnp.logical_and(own, x == i)))
            def _():
                do(direct(i, h))

        for h in ORDER:
            @pl.when(second_root)
            def _():
                for i in range(PIECES):
                    both(1, i, h, second_copy, own_second)

            @pl.when(first_root)
            def _():
                for i in range(PIECES):
                    both(0, i, h, first_copy, own_first)

    def keep(condition, source, target, do):
        @pl.when(condition)
        def _():
            do(pltpu.make_async_copy(source, target, local_sem.at[2]))

    def keep_first(do):
        keep(own_first, stage.at[0, x], left.at[0, x], do)

    def keep_second(do):
        keep(own_second, stage.at[1, x], onward, do)

    def first_meta(peer):
        return remote(meta, metas.at[0], meta_send.at[0], meta_recv.at[0], *peer)

    def second_meta(peer):
        return remote(meta, metas.at[1], meta_send.at[1], meta_recv.at[1], *peer)

    def home_meta(peer):
        return remote(meta, root_meta, meta_send.at[4], meta_recv.at[4], *peer)

    shift_meta = remote(meta, metas.at[2], meta_send.at[2], meta_recv.at[2], below, c)
    if partial:
        upward_meta = remote(meta, below_meta, meta_send.at[3], meta_recv.at[3], above, c)

    def sent(n, send):
        many = z_flags.at[pl.ds(0, n)]
        remote(many, many, send, flag_recv.at[0], below, c).wait_send()

    slots = ROOM if partial else SLOTS
    parts = 2 if partial else 5

    def shift_copy(i):
        part = pl.ds(i * (slots // parts), slots // parts)
        source = packed if partial else blocks
        return remote(source.at[part], right.at[part], shift_send.at[i], shift_recv.at[i], below, c)

    def straight_first(h):
        return pass_on(0, x, h, cross_sem.at[h], r, other)

    def straight_second(h):
        return pass_on(1, x, h, cross_sem.at[h], below, other, chunk(onward, h))

    def to_near(h):
        return pass_on(1, x, h, near_sem.at[h], below, same, chunk(onward, h))

    def from_aside(role, h):
        return pass_on(role, x, h, cross_sem.at[h], aside_of if role == 0 else across_below, other, chunk(aside, h))

    def x_copy(n, h):
        return pass_on(k, x, h, x_sem.at[n, h], r, at(ring[n], k))

    def core_copy(n, i, h):
        return pass_on(k, i, h, core_sem.at[n, h], r, at(x, 1 - k))

    def arrived(panel, i, h):
        pass_on(panel, i, h, core_sem.at[0, 0], r, at(x, 1 - k)).wait_recv()

    def landed(ref, h, sem):
        remote(chunk(ref, h), chunk(ref, h), core_sem.at[0, 0], sem.at[h], r, at(x, 1 - k)).wait_recv()

    def amount(condition, n):
        return jnp.where(condition, n, 0)

    sends = (
        5
        + amount(first_root, 8 + 15) - amount(own_first, 1)
        + amount(second_root, 8 + 16) - amount(own_second, 1)
        + amount(near_first, 1) + amount(aside_first, 1) + amount(near_second, 2) + amount(aside_second, 1)
    )
    if partial:
        sends = sends + 1 + 25 + amount(second_root, 15)
    pl.semaphore_wait(barrier, sends)

    if partial:
        upward_meta.start()

        @pl.when(second_root)
        def _():
            for peer in row_peers:
                home_meta(peer).start()
            root_meta[...] = meta[...]

    for_root_copies(lambda copy: copy.start())
    keep_first(lambda copy: copy.start())
    keep_second(lambda copy: copy.start())
    shift_meta.start()

    if not partial:
        for i in range(parts):
            shift_copy(i).start()

    @pl.when(first_root)
    def _():
        for peer in row_peers:
            first_meta(peer).start()
        metas[0] = meta[...]

    @pl.when(second_root)
    def _():
        for col in range(N_COL):
            second_meta((below, col)).start()

    keep_first(lambda copy: copy.wait())
    keep_second(lambda copy: copy.wait())

    def spread(h):
        for n in range(3):
            x_copy(n, h).start()
        core_copy(0, x, h).start()

    @pl.when(near_first)
    def _():
        for h in ORDER:
            @pl.when(jnp.logical_not(own_first))
            def _():
                arrived(0, x, h)

            if h in STRAIGHT:
                straight_first(h).start()

    @pl.when(aside_first)
    def _():
        for h in ASIDE:
            landed(aside, h, aside_sem)
            from_aside(0, h).start()

    @pl.when(near_second)
    def _():
        for h in ORDER:
            @pl.when(jnp.logical_not(own_second))
            def _():
                landed(onward, h, onward_sem)

            if h in STRAIGHT:
                straight_second(h).start()
        for h in ORDER:
            to_near(h).start()

    @pl.when(aside_second)
    def _():
        for h in ASIDE:
            landed(aside, h, aside_sem)
            from_aside(1, h).start()

    def send_flags(peers, buffer, me, n):
        buffer[me] = flag_v[n]
        for peer in peers:
            remote(flag_v.at[n], buffer.at[me], flag_send.at[n], flag_recv.at[n], *peer).start()

    def join_flags(buffer, count, n):
        others = buffer.at[pl.ds(0, count - 1)]
        remote(others, others, flag_send.at[n], flag_recv.at[n], below, c).wait_recv()
        joined = buffer[0]
        for i in range(1, count):
            joined = jnp.maximum(joined, buffer[i])
        return joined

    wide_lane = lax.broadcasted_iota(jnp.int32, (SLOTS, 128), 1)
    wide_sub = lax.broadcasted_iota(jnp.int32, (SLOTS, 128), 0)

    line, column = own[0:1, :], own[1:2, :]

    def down(values):
        return jnp.sum(jnp.where(wide_lane == wide_sub, values, 0), axis=1, keepdims=True)

    def bits(rows, valid):
        return jnp.where(valid, jnp.left_shift(1, jnp.maximum(rows, 0)), 0)

    def union(keys, masks, wanted):
        return jnp.sum(jnp.where(down(keys) == wanted, down(masks), 0), axis=0, keepdims=True)

    def rank(chosen):
        return jnp.sum(jnp.where(wide_sub < wide_lane, down(jnp.where(chosen, 1, 0)), 0), axis=0, keepdims=True)

    def left_half(coords, which):
        lines, columns = coords[0:1, :], coords[1:2, :] - BROW * which
        inside = jnp.logical_and(lines >= 0, jnp.logical_and(columns >= 0, columns < BROW))
        return lines, jnp.where(inside, columns, -1), inside

    def needs_of(lines, columns, half_coords, output_lines, output_columns):
        left_lines, left_columns, inside = half_coords
        by_line = union(left_lines, bits(left_columns, inside), lines)
        by_column = union(output_columns, bits(output_lines, output_lines >= 0), columns)
        return jnp.logical_and(lines >= 0, jnp.bitwise_and(by_line, by_column) != 0)

    if partial:
        upward_meta.wait_recv()

        @pl.when(jnp.logical_not(second_root))
        def _():
            home_meta(row_peers[0]).wait_recv()

        theirs = below_meta[...]
        needed = needs_of(line, column, left_half(root_meta[...], below % 2), theirs[0:1, :], theirs[1:2, :])
        spot_sub = lax.broadcasted_iota(jnp.int32, (ROOM, 128), 0)
        spot_lane = lax.broadcasted_iota(jnp.int32, (ROOM, 128), 1)
        chosen = jnp.logical_and(needed, rank(needed) == spot_sub)
        slot = jnp.sum(jnp.where(chosen, spot_lane, 0), axis=1, keepdims=True)
        need_v[...] = jnp.broadcast_to(slot, (ROOM, 128))
        needs = pltpu.make_async_copy(need_v, need_s, local_sem.at[3])
        needs.start()
        total = jnp.sum(jnp.where(needed, 1, 0), axis=1, keepdims=True)
        flag_v[0] = jnp.broadcast_to(jnp.where(total > ROOM, 1, 0), (8, 128))
        needs.wait()
        for s in range(ROOM):
            packed[s] = held[jnp.clip(need_s[s, 0], 0, SLOTS - 1)]
        shift_copy(0).start()
        send_flags(chip_peers, chip_flags, x * 2 + k, 0)

    if partial:
        flag_v[1] = join_flags(chip_flags, 8, 0)
        send_flags(z_peers, z_flags, z, 1)

    for h in ORDER:
        @pl.when(jnp.logical_not(near_first))
        def _():
            arrived(k, x, h)

        spread(h)

    if partial:
        shift_copy(1).start()
        flag_v[2] = join_flags(z_flags, 16, 1)
        send_flags(y_peers, y_flags, y, 2)

    for h in ORDER:
        for n in range(3):
            arrived(k, ring[n], h)
            core_copy(1 + n, ring[n], h).start()

    @pl.when(jnp.logical_not(first_root))
    def _():
        first_meta(row_peers[0]).wait_recv()

    second_meta((below, c)).wait_recv()
    shift_meta.wait_recv()
    halves = [left_half(metas[p], r % 2) for p in range(2)]
    shift_line, shift_column = metas[2, 0:1, :], metas[2, 1:2, :]
    if partial:
        present = needs_of(shift_line, shift_column, halves[1], line, column)
        position = jnp.minimum(rank(present), ROOM - 1)
    else:
        present = shift_line >= 0
        position = lane[0:1, :]
    entries = []
    for p, (lines, columns) in enumerate(((line, column), (shift_line, shift_column))):
        left_lines, left_columns, inside = halves[p]
        meet = jnp.bitwise_and(
            union(left_columns, bits(left_lines, inside), line), union(columns, bits(lines, lines >= 0), column)
        )
        entries.append(jnp.where(line >= 0, meet, 0))
        entries.append(jnp.where(inside, p * 256 + left_columns * 16 + left_lines, 255))
        entries.append(jnp.minimum(rank(inside), HALF - 1))
    entries.append(jnp.where(line >= 0, column * 16 + line, 511))
    entries.append(jnp.where(present, 512 + shift_column * 16 + shift_line, 1023))
    entries.append(position)
    entries.append(jnp.maximum(line, 0) * 16)
    entries.append(jnp.maximum(column, 0) * 16)
    sub16 = lax.broadcasted_iota(jnp.int32, (16, 128), 0)
    table = jnp.zeros((16, 128), jnp.int32)
    for i, entry in enumerate(entries):
        table = jnp.where(sub16 == i, entry, table)
    plan_v[...] = table
    plan_out = pltpu.make_async_copy(plan_v, plan, local_sem.at[1])
    plan_out.start()

    for h in ORDER:
        for i in range(PIECES):
            arrived(1 - k, i, h)

    if partial:
        flag[0, 0] = jnp.max(join_flags(y_flags, 4, 2))
        sent(7, flag_send.at[0])
        sent(15, flag_send.at[1])
        sent(3, flag_send.at[2])
    else:
        flag[0, 0] = 0

    plan_out.wait()
    for_root_copies(lambda copy: copy.wait_send())

    @pl.when(first_root)
    def _():
        sent(15, meta_send.at[0])

    @pl.when(second_root)
    def _():
        sent(16, meta_send.at[1])

    shift_meta.wait_send()
    if partial:
        upward_meta.wait_send()

        @pl.when(second_root)
        def _():
            sent(15, meta_send.at[4])

    @pl.when(near_first)
    def _():
        for h in STRAIGHT:
            straight_first(h).wait_send()

    @pl.when(near_second)
    def _():
        for h in STRAIGHT:
            straight_second(h).wait_send()
        for h in ORDER:
            to_near(h).wait_send()

    @pl.when(aside_first)
    def _():
        for h in ASIDE:
            from_aside(0, h).wait_send()

    @pl.when(aside_second)
    def _():
        for h in ASIDE:
            from_aside(1, h).wait_send()

    for h in ORDER:
        for n in range(3):
            x_copy(n, h).wait_send()
        core_copy(0, x, h).wait_send()
        for n in range(3):
            core_copy(1 + n, ring[n], h).wait_send()
    for i in range(parts):
        shift_copy(i).wait()


def gather(rows, cols, blocks, partial):
    any_space = pl.BlockSpec(memory_space=pl.ANY)
    scalars = pl.BlockSpec(memory_space=pltpu.SMEM)
    dma = pltpu.SemaphoreType.DMA
    tile = (8, 128)
    hops = len(CHUNKS)
    return pl.pallas_call(
        functools.partial(gather_kernel, partial),
        name="gather_needed" if partial else "gather_all",
        out_shape=(
            jax.ShapeDtypeStruct((2, PIECES, PIECE_ROWS, BS), jnp.bfloat16),
            jax.ShapeDtypeStruct((ROOM if partial else SLOTS, BS, BS), jnp.bfloat16),
            jax.ShapeDtypeStruct((16, 128), jnp.int32),
            jax.ShapeDtypeStruct((1, 1), jnp.int32),
        ),
        in_specs=[scalars, scalars, any_space],
        out_specs=(any_space, any_space, any_space, scalars),
        scratch_shapes=[
            pltpu.VMEM((16, 128), jnp.int32),
            pltpu.VMEM((3, *tile), jnp.int32),
            pltpu.VMEM((SLOTS, BS, BS), jnp.bfloat16),
            pltpu.VMEM((2, PIECES, PIECE_ROWS, BS), jnp.bfloat16),
            pltpu.VMEM((ROOM, BS, BS), jnp.bfloat16),
            pltpu.VMEM(tile, jnp.int32),
            pltpu.VMEM(tile, jnp.int32),
            pltpu.VMEM(tile, jnp.int32),
            pltpu.VMEM(tile, jnp.int32),
            pltpu.SMEM(tile, jnp.int32),
            pltpu.VMEM((ROOM, 128), jnp.int32),
            pltpu.SMEM((ROOM, 128), jnp.int32),
            pltpu.VMEM((PIECE_ROWS, BS), jnp.bfloat16),
            pltpu.VMEM((PIECE_ROWS, BS), jnp.bfloat16),
            pltpu.VMEM((8, *tile), jnp.int32),
            pltpu.VMEM((16, *tile), jnp.int32),
            pltpu.VMEM((4, *tile), jnp.int32),
            pltpu.VMEM((3, *tile), jnp.int32),
            dma((4,)),
            dma((2, 2, PIECES, hops)),
            dma((2, PIECES, hops)),
            dma((hops,)),
            dma((hops,)),
            dma((hops,)),
            dma((hops,)),
            dma((3, hops)),
            dma((PIECES, hops)),
            dma((5,)),
            dma((5,)),
            dma((5,)),
            dma((5,)),
            dma((3,)),
            dma((3,)),
        ],
        compiler_params=pltpu.CompilerParams(
            collective_id=0 if partial else 1, has_side_effects=True, vmem_limit_bytes=GATHER_MIB * 1024 * 1024
        ),
    )(rows, cols, blocks)


GATHER_MIB = 62
MULTIPLY_MIB = 62


MEET, LEFT_CELL, LEFT_PLACE = (0, 3), (1, 4), (2, 5)
OWN_CELL, SHIFT_CELL, SHIFT_PLACE, LEFT_BASE, RIGHT_BASE = 6, 7, 8, 9, 10
LOWEST = 0x09AF


def multiply_kernel(
    plan, blocks, right, left, out,
    left_slot, right_slot, bit_s, where_s, slot_s, count_s,
    zeros, left_v, right_v, total, done, zero_sem, load_sem, store_sem,
):
    zeros[...] = jnp.zeros_like(zeros)
    clear = pltpu.make_async_copy(zeros, out, zero_sem)
    clear.start()
    for i in range(16):
        bit_s[(LOWEST << i & 0xFFFF) >> 12] = i
    count_s[0] = 0
    count_s[1] = 0

    @pl.loop(0, SLOTS, unroll=8)
    def _(t):
        for p in range(2):
            left_slot[plan[LEFT_CELL[p], t]] = plan[LEFT_PLACE[p], t]
        right_slot[plan[OWN_CELL, t]] = t
        right_slot[plan[SHIFT_CELL, t]] = plan[SHIFT_PLACE, t]

    def load(p, m, t):
        n = jnp.minimum(count_s[0], MEETINGS - 1)
        j = jnp.clip(left_slot[p * 256 + plan[LEFT_BASE, t] + m], 0, HALF - 1)
        piece = j // PER
        start = pl.multiple_of((j - piece * PER) * BS, BS)
        source = (blocks, right)[p]
        slot = jnp.clip(right_slot[p * 512 + plan[RIGHT_BASE, t] + m], 0, source.shape[0] - 1)
        pltpu.make_async_copy(left.at[p, piece, pl.ds(start, BS)], left_v.at[n], load_sem.at[0]).start()
        pltpu.make_async_copy(source.at[slot], right_v.at[n], load_sem.at[1]).start()
        where_s[n] = t
        count_s[0] = n + 1

    @pl.loop(0, SLOTS)
    def _(t):
        meet = [plan[MEET[p], t] for p in range(2)]

        @pl.when((meet[0] | meet[1]) != 0)
        def _():
            slot_s[count_s[1]] = t
            count_s[1] = count_s[1] + 1
            total[t] = jnp.zeros_like(total[t])
            for p in range(2):
                def each(bits):
                    lowest = bits & -bits
                    load(p, bit_s[((lowest * LOWEST) & 0xFFFF) >> 12], t)
                    return bits ^ lowest

                lax.while_loop(lambda bits: bits != 0, each, meet[p])

    n, slots = count_s[0], count_s[1]
    for u in range(GROUP):
        where_s[n + u] = SLOTS

    @pl.loop(0, n)
    def _(i):
        pltpu.make_async_copy(blocks.at[0], left_v.at[0], load_sem.at[0]).wait()
        pltpu.make_async_copy(blocks.at[0], right_v.at[0], load_sem.at[1]).wait()

    @pl.loop(0, (n + GROUP - 1) // GROUP)
    def _(g):
        products = [
            jnp.dot(left_v[g * GROUP + u], right_v[g * GROUP + u], preferred_element_type=jnp.float32)
            for u in range(GROUP)
        ]
        for u in range(GROUP):
            t = where_s[g * GROUP + u]
            total[t] = total[t] + products[u]

    clear.wait()

    @pl.loop(0, slots)
    def _(i):
        t = slot_s[i]
        done[i] = total[t].astype(jnp.bfloat16)
        pltpu.make_async_copy(done.at[i], out.at[t], store_sem).start()

    @pl.loop(0, slots)
    def _(i):
        pltpu.make_async_copy(done.at[0], out.at[0], store_sem).wait()


def multiply(plan, blocks, right, left):
    any_space = pl.BlockSpec(memory_space=pl.ANY)
    room = MEETINGS + GROUP
    return pl.pallas_call(
        multiply_kernel,
        name="multiply",
        out_shape=jax.ShapeDtypeStruct((SLOTS, BS, BS), jnp.bfloat16),
        in_specs=[pl.BlockSpec(memory_space=pltpu.SMEM), any_space, any_space, any_space],
        out_specs=any_space,
        scratch_shapes=[
            pltpu.SMEM((512,), jnp.int32),
            pltpu.SMEM((1024,), jnp.int32),
            pltpu.SMEM((16,), jnp.int32),
            pltpu.SMEM((room,), jnp.int32),
            pltpu.SMEM((SLOTS,), jnp.int32),
            pltpu.SMEM((2,), jnp.int32),
            pltpu.VMEM((SLOTS, BS, BS), jnp.bfloat16),
            pltpu.VMEM((room, BS, BS), jnp.bfloat16),
            pltpu.VMEM((room, BS, BS), jnp.bfloat16),
            pltpu.VMEM((SLOTS + 1, BS, BS), jnp.float32),
            pltpu.VMEM((SLOTS, BS, BS), jnp.bfloat16),
            pltpu.SemaphoreType.DMA,
            pltpu.SemaphoreType.DMA((2,)),
            pltpu.SemaphoreType.DMA,
        ],
        compiler_params=pltpu.CompilerParams(vmem_limit_bytes=MULTIPLY_MIB * 1024 * 1024),
    )(plan, blocks, right, left)


def product(rows, cols, blocks, partial):
    left, right, plan, flag = gather(rows, cols, blocks, partial)
    return multiply(plan, blocks, right, left), flag


def shards(blocks, block_rows, block_cols):
    blocks, rows, cols = blocks[0, 0], block_rows[0, 0], block_cols[0, 0]
    result, flag = product(rows, cols, blocks, True)
    result = lax.cond(flag[0, 0] > 0, lambda: product(rows, cols, blocks, False)[0], lambda: result)
    return result[None, None]


def solution(mesh):
    return jax.shard_map(
        shards,
        mesh=mesh,
        in_specs=(P("row", "col", None, None, None), P("row", "col", None), P("row", "col", None)),
        out_specs=P("row", "col", None, None, None),
        check_vma=False,
    )
```
